32 devices in a mesh: radial: 8 (over y, x, core), axial: 4 (over z).
Axes of the slice: x: 2, y: 2, z: 4, core: 2. Of those that a mesh axis runs over, the one named last changes fastest.
Arguments:
- rhs: float32 [2, 2, 96, 64, 512], P(None, None, None, 'radial', 'axial'), may hold values from -6 to 6
- mat_ids: int32 [96, 64, 512], P(None, 'radial', 'axial'), may hold values from 0 to 3
- stiff_table: float32 [4], replicated, may hold values from 0.5 to 4
- dens_table: float32 [4], replicated, may hold values from 0.5 to 2
- mass_shift: float32 [2], replicated, may hold values from 0.5 to 2
- harmonic: int32 [2], replicated, may hold values from 1 to 12
- radial_factor: float32 [2, 2, 16, 16], replicated, may hold values from -0.09375 to 0.09375
- axial_factor: float32 [2, 2, 64, 64], replicated, may hold values from -0.046875 to 0.046875
Outputs:
- solution: float32 [2, 2, 96, 64, 512], P(None, None, None, 'radial', 'axial')
- residual: float32 [2, 2, 96, 64, 512], P(None, None, None, 'radial', 'axial')
The draws below stay inside these ranges and needn't reach their ends.
All inputs are finite; a program needn't handle non-finite values.
Results may differ from the reference program's by a relative error of at most 0.00021.
Values sent between devices are 32-bit elements; how exact they have to be, the bound alone decides.
A program may use at most 128 MiB of HBM per device.

```python
import math
import jax
import jax.numpy as jnp
from jax import lax

CT = 96
HARM = 2
ITERS = 3
NSECT = 24
NMAT = 4
AR = 4
AA = 8
NR = 64
NA = 512
GR = 16
GA = 64


def touch_ends(values, stream_key, low, top_value):
    longest = values.shape.index(max(values.shape))
    spots = []
    for shift in (0, 1):
        where = [jax.random.randint(jax.random.fold_in(stream_key, axis), (), 0, length) for axis, length in enumerate(values.shape)]
        where[longest] = (where[longest] + shift) % values.shape[longest]
        spots.append(tuple(where))
    return values.at[spots[0]].set(low).at[spots[1]].set(top_value)


def steps_of(rng, shape, cuts, low, largest):
    def one(position, blocks):
        steps = jax.random.uniform(jax.random.fold_in(jax.random.fold_in(rng, 6), position), (blocks,), jnp.float32, low / len(cuts), largest / len(cuts))
        return jnp.repeat(jnp.exp(steps), shape[position] // blocks).reshape((-1,) + (1,) * (len(shape) - position - 1))

    level = one(*cuts[0])
    for cut in cuts[1:]:
        level = level * one(*cut)
    return level


def normal_values(rng, shape, scale, reach, pieces=(), kind=jnp.bfloat16):
    gain = steps_of(rng, shape, pieces, -0.22, 0.18) if pieces else 1.0
    entries = jax.random.normal(rng, shape, jnp.float32) * scale * gain
    return jnp.minimum(jnp.maximum(entries, -reach), reach).astype(kind)


def setup_inputs(seed: int = 0) -> dict:
    splits = jax.random.split(jax.random.key(seed), 9)
    rhs = normal_values(splits[0], (2, HARM, CT, NR, NA), 1.0, 6.0, ((3, 8), (4, 4)), jnp.float32)
    mat_ids = touch_ends(jax.random.randint(splits[1], (CT, NR, NA), 0, NMAT), jax.random.fold_in(splits[1], 1), 0, NMAT - 1).astype(jnp.int32)
    stiff_table = jnp.clip(jnp.exp(jax.random.uniform(splits[2], (NMAT,), jnp.float32, math.log(0.5), math.log(4.0))), 0.5, 4.0)
    dens_table = jnp.clip(jnp.exp(jax.random.uniform(splits[3], (NMAT,), jnp.float32, math.log(0.5), math.log(2.0))), 0.5, 2.0)
    mass_shift = jnp.clip(jax.random.uniform(splits[4], (HARM,), jnp.float32, 0.5, 2.0), 0.5, 2.0)
    harmonic = jax.random.randint(splits[5], (HARM,), 1, NSECT // 2 + 1).astype(jnp.int32)
    radial_factor = normal_values(splits[6], (2, HARM, GR, GR), (256 * GR) ** -0.5, 0.09375, (), jnp.float32)
    axial_factor = normal_values(splits[7], (2, HARM, GA, GA), (256 * GA) ** -0.5, 0.046875, (), jnp.float32)
    return {"rhs": rhs, "mat_ids": mat_ids, "stiff_table": stiff_table, "dens_table": dens_table, "mass_shift": mass_shift, "harmonic": harmonic, "radial_factor": radial_factor, "axial_factor": axial_factor}


LOSS_FACTOR = 0.2
RELAXATION = 0.6


def material(mat_ids, table):
    result = jnp.zeros(mat_ids.shape, table.dtype)
    for entry in range(table.shape[0]):
        result = result + jnp.where(mat_ids == entry, table[entry], jnp.zeros((), table.dtype))
    return result


def couplings(stiffness, padded):
    return (0.5 * (stiffness + padded[:, 2:, 1:-1]),
            0.5 * (stiffness + padded[:, :-2, 1:-1]),
            0.5 * (stiffness + padded[:, 1:-1, 2:]),
            0.5 * (stiffness + padded[:, 1:-1, :-2]),
            0.5 * (stiffness + jnp.roll(stiffness, -1, 0)),
            0.5 * (stiffness + jnp.roll(stiffness, 1, 0)))


def neighbours(values, padded, weights, cosines, sines):
    summed = weights[0] * padded[:, :, :, 2:, 1:-1] + weights[1] * padded[:, :, :, :-2, 1:-1]
    summed = summed + weights[2] * padded[:, :, :, 1:-1, 2:] + weights[3] * padded[:, :, :, 1:-1, :-2]
    real_part = values[0]
    imag_part = values[1]
    cosine = cosines[:, None, None, None]
    sine = sines[:, None, None, None]
    wrap_real = cosine * real_part[:, :1] - sine * imag_part[:, :1]
    wrap_imag = sine * real_part[:, :1] + cosine * imag_part[:, :1]
    ahead = jnp.stack([jnp.concatenate([real_part[:, 1:], wrap_real], 1),
                       jnp.concatenate([imag_part[:, 1:], wrap_imag], 1)])
    back_real = cosine * real_part[:, -1:] + sine * imag_part[:, -1:]
    back_imag = cosine * imag_part[:, -1:] - sine * real_part[:, -1:]
    behind = jnp.stack([jnp.concatenate([back_real, real_part[:, :-1]], 1),
                        jnp.concatenate([back_imag, imag_part[:, :-1]], 1)])
    return summed + weights[4] * ahead + weights[5] * behind


def operate(values, padded, weights, diag_real, diag_imag, cosines, sines):
    coupled = neighbours(values, padded, weights, cosines, sines)
    real_out = diag_real * values[0] - diag_imag * values[1] - (coupled[0] - LOSS_FACTOR * coupled[1])
    imag_out = diag_real * values[1] + diag_imag * values[0] - (coupled[1] + LOSS_FACTOR * coupled[0])
    return jnp.stack([real_out, imag_out])


def right_product(left_real, left_imag, right_real, right_imag):
    def matmul(first, second):
        return jnp.einsum('hij,hkj->hik', first, second, precision=lax.Precision.HIGHEST)
    return (matmul(left_real, right_real) - matmul(left_imag, right_imag),
            matmul(left_real, right_imag) + matmul(left_imag, right_real))


def left_product(left_real, left_imag, right_real, right_imag):
    def matmul(first, second):
        return jnp.einsum('hij,hjk->hik', first, second, precision=lax.Precision.HIGHEST)
    return (matmul(left_real, right_real) - matmul(left_imag, right_imag),
            matmul(left_real, right_imag) + matmul(left_imag, right_real))


def jacobi_step(residual, diag_real, diag_imag):
    scale = RELAXATION / (diag_real * diag_real + diag_imag * diag_imag)
    real_out = (diag_real * residual[0] + diag_imag * residual[1]) * scale
    imag_out = (diag_real * residual[1] - diag_imag * residual[0]) * scale
    return jnp.stack([real_out, imag_out])


def restrict(residual, rows, cols):
    shape = residual.shape
    blocks = residual.reshape(2, shape[1], shape[2], rows, AR, cols, AA)
    return jnp.sum(blocks, axis=(2, 4, 6))


def prolong(coarse_values):
    spread = jnp.repeat(jnp.repeat(coarse_values, AR, axis=2), AA, axis=3)
    return spread[:, :, None]


def pad_field(values):
    return jnp.pad(values, ((0, 0), (0, 0), (0, 0), (1, 1), (1, 1)))


def reference(rhs, mat_ids, stiff_table, dens_table, mass_shift, harmonic, radial_factor, axial_factor):
    stiffness = material(mat_ids, stiff_table)
    density = material(mat_ids, dens_table)
    padded_stiff = jnp.pad(stiffness, ((0, 0), (1, 1), (1, 1)))
    weights = couplings(stiffness, padded_stiff)
    total = weights[0] + weights[1] + weights[2] + weights[3] + weights[4] + weights[5]
    diag_real = total[None] - mass_shift[:, None, None, None] * density[None]
    diag_imag = LOSS_FACTOR * total
    angles = (2.0 * jnp.pi / NSECT) * harmonic.astype(rhs.dtype)
    cosines = jnp.cos(angles)
    sines = jnp.sin(angles)
    solution = jnp.zeros_like(rhs)
    residual = rhs
    for iteration in range(ITERS):
        if iteration > 0:
            residual = rhs - operate(solution, pad_field(solution), weights, diag_real, diag_imag, cosines, sines)
        coarse_res = restrict(residual, GR, GA)
        mixed_real, mixed_imag = right_product(coarse_res[0], coarse_res[1], axial_factor[0], axial_factor[1])
        corr_real, corr_imag = left_product(radial_factor[0], radial_factor[1], mixed_real, mixed_imag)
        solution = solution + jacobi_step(residual, diag_real, diag_imag) + prolong(jnp.stack([corr_real, corr_imag]))
    residual = rhs - operate(solution, pad_field(solution), weights, diag_real, diag_imag, cosines, sines)
    return solution, residual
```

```python
import functools

import jax
import jax.numpy as jnp
from jax import lax
from jax.experimental import pallas as pl
from jax.experimental.pallas import tpu as pltpu
from jax.sharding import PartitionSpec as P

ITERS = 3
NSECT = 24
AR = 4
AA = 8
LOSS_FACTOR = 0.2
RELAXATION = 0.6
MESH = pl.DeviceIdType.MESH
HIGHEST = lax.Precision.HIGHEST


def kernel(
    nrad,
    nax,
    rhs_ref,
    ids_ref,
    stiff_ref,
    dens_ref,
    mass_ref,
    harm_ref,
    radial_ref,
    axial_ref,
    sol_ref,
    res_ref,
    stiff,
    wr_up,
    wr_dn,
    wa_lo,
    wa_hi,
    wt,
    dr,
    di,
    sc,
    srow_s,
    srow_r,
    scol_s,
    scol_r,
    row_s,
    row_r,
    col_s,
    col_r,
    one_s,
    one_r,
    two_r,
    axmat,
    radmat,
    st_send,
    st_recv,
    ha_send,
    ha_recv,
    g1_send,
    g1_recv,
    g2_send,
    g2_recv,
):
    ct = rhs_ref.shape[2]
    rows, lanes = rhs_ref.shape[3:]
    gr = radial_ref.shape[2]
    ga = axial_ref.shape[2]
    band_r = rows // AR
    band_c = lanes // AA
    i = lax.axis_index("radial")
    j = lax.axis_index("axial")
    has_up, has_dn = i > 0, i < nrad - 1
    has_lo, has_hi = j > 0, j < nax - 1
    conds = (has_up, has_dn, has_lo, has_hi)
    targets = ({"radial": i - 1}, {"radial": i + 1}, {"axial": j - 1}, {"axial": j + 1})

    for d in range(4):

        @pl.when(jnp.logical_not(conds[d]))
        def _():
            if d < 2:
                srow_r[d] = jnp.zeros(srow_r.shape[1:], jnp.float32)
                for k in range(ITERS):
                    row_r[k, d] = jnp.zeros(row_r.shape[2:], jnp.float32)
            else:
                scol_r[d - 2] = jnp.zeros(scol_r.shape[1:], jnp.float32)
                for k in range(ITERS):
                    col_r[k, d - 2] = jnp.zeros(col_r.shape[2:], jnp.float32)

    barrier = pltpu.get_barrier_semaphore()
    for d in range(1, nax):
        pl.semaphore_signal(
            barrier, inc=1, device_id={"axial": lax.rem(j + d, nax)}, device_id_type=MESH
        )
    for d in range(1, nrad):
        pl.semaphore_signal(
            barrier, inc=1, device_id={"radial": lax.rem(i + d, nrad)}, device_id_type=MESH
        )

    row = lax.broadcasted_iota(jnp.int32, (rows, lanes), 0)
    lane = lax.broadcasted_iota(jnp.int32, (rows, lanes), 1)
    zero = jnp.zeros((rows, lanes), jnp.float32)

    def lookup(ids, table):
        value = jnp.full(ids.shape, table[0], jnp.float32)
        for entry in range(1, table.shape[0]):
            value = jnp.where(ids == entry, table[entry], value)
        return value

    def pack(value, t, first, last):
        first = jnp.where(lane == t, pltpu.roll(value, t, 1), first)
        last = jnp.where(lane == t, pltpu.roll(value, t + 1, 1), last)
        return first, last

    def stiff_copy(d):
        if d < 2:
            src, dst = srow_s.at[d], srow_r.at[1 - d]
        else:
            src, dst = scol_s.at[d - 2], scol_r.at[3 - d]
        return pltpu.make_async_remote_copy(
            src_ref=src,
            dst_ref=dst,
            send_sem=st_send.at[d],
            recv_sem=st_recv.at[d ^ 1],
            device_id=targets[d],
            device_id_type=MESH,
        )

    def halo_copy(k, d):
        if d < 2:
            src, dst = row_s.at[k, d], row_r.at[k, 1 - d]
        else:
            src, dst = col_s.at[k, d - 2], col_r.at[k, 3 - d]
        return pltpu.make_async_remote_copy(
            src_ref=src,
            dst_ref=dst,
            send_sem=ha_send.at[k, d],
            recv_sem=ha_recv.at[k, d ^ 1],
            device_id=targets[d],
            device_id_type=MESH,
        )

    def gather_one(k, d):
        return pltpu.make_async_remote_copy(
            src_ref=one_s.at[k],
            dst_ref=one_r.at[k, j],
            send_sem=g1_send.at[k, d],
            recv_sem=g1_recv.at[k, d],
            device_id={"axial": lax.rem(j + d, nax)},
            device_id_type=MESH,
        )

    def gather_two(k, d):
        return pltpu.make_async_remote_copy(
            src_ref=two_r.at[k, i],
            dst_ref=two_r.at[k, i],
            send_sem=g2_send.at[k, d],
            recv_sem=g2_recv.at[k, d],
            device_id={"radial": lax.rem(i + d, nrad)},
            device_id_type=MESH,
        )

    def on_faces(act):
        for d in range(4):

            @pl.when(conds[d])
            def _():
                act(d)

    def first_pass(t, carry):
        first, last, s0, s1, s2, s3 = carry
        value = lookup(ids_ref[t], stiff_ref)
        stiff[t + 1] = value
        srow_s[0, pl.ds(t, 1), :] = value[0:1]
        srow_s[1, pl.ds(t, 1), :] = value[rows - 1 : rows]
        first, last = pack(value, t, first, last)
        return (
            first,
            last,
            s0 + rhs_ref[0, 0, t],
            s1 + rhs_ref[0, 1, t],
            s2 + rhs_ref[1, 0, t],
            s3 + rhs_ref[1, 1, t],
        )

    first, last, *sums = lax.fori_loop(0, ct, first_pass, (zero,) * 6)
    scol_s[0] = first
    scol_s[1] = last
    stiff[0] = stiff[ct]
    stiff[ct + 1] = stiff[1]

    pl.semaphore_wait(barrier, nax + nrad - 2)
    on_faces(lambda d: stiff_copy(d).start())

    e_row = lax.broadcasted_iota(jnp.int32, (lanes, lanes), 0)
    e_col = lax.broadcasted_iota(jnp.int32, (lanes, lanes), 1)
    fold = jnp.where(e_row // AA + j * band_c == e_col, 1.0, 0.0)

    def restrict_and_send(k, sums):
        tile = zero
        for c in range(4):
            s = sums[c] + pltpu.roll(sums[c], rows - 1, 0)
            s = s + pltpu.roll(s, rows - 2, 0)
            for g in range(band_r):
                to = c * band_r + g
                moved = pltpu.roll(s, (to - g * AR) % rows, 0)
                tile = jnp.where(row == to, moved, tile)
        one_s[k] = jnp.dot(tile, fold, precision=HIGHEST, preferred_element_type=jnp.float32)
        for d in range(1, nax):
            gather_one(k, d).start()

    restrict_and_send(0, sums)

    ax_row = lax.broadcasted_iota(jnp.int32, (lanes, ga), 0)
    ax_col = lax.broadcasted_iota(jnp.int32, (lanes, ga), 1)
    own = jnp.where(ax_row // AA + j * band_c == ax_col, 1.0, 0.0)
    edge_lo = j * band_c - 1
    edge_hi = (j + 1) * band_c
    half = lanes // 2
    edges = []
    for p in range(2):
        hit = ((ax_row == p * half) & (ax_col == edge_lo)) | (
            (ax_row == p * half + 1) & (ax_col == edge_hi)
        )
        edges.append(jnp.where(hit, 1.0, 0.0))
    for h in range(2):
        if ga < lanes:
            axmat[h] = jnp.zeros(axmat.shape[1:], jnp.float32)

        def spread(select, p):
            return jnp.dot(
                select, axial_ref[p, h], precision=HIGHEST, preferred_element_type=jnp.float32
            )

        axmat[h, 0:lanes, 0:ga] = spread(own, 0)
        axmat[h, lanes : 2 * lanes, 0:ga] = spread(own, 1)
        axmat[h, 2 * lanes : 3 * lanes, 0:ga] = spread(edges[0], 0) + spread(edges[1], 1)

    per = 2 * rows
    cdev = 4 * band_r
    r_row = lax.broadcasted_iota(jnp.int32, (4 * per, gr), 0) % per
    r_col = lax.broadcasted_iota(jnp.int32, (4 * per, gr), 1)
    want = jnp.where(
        r_row < rows,
        r_row // AR + i * band_r,
        jnp.where(
            r_row == rows, i * band_r - 1, jnp.where(r_row == rows + 1, (i + 1) * band_r, -1)
        ),
    )
    r_sel = jnp.where(want == r_col, 1.0, 0.0)
    c_row = lax.broadcasted_iota(jnp.int32, (gr, nrad * cdev), 0)
    c_col = lax.broadcasted_iota(jnp.int32, (gr, nrad * cdev), 1)
    c_sel = jnp.where((c_col // cdev) * band_r + c_col % band_r == c_row, 1.0, 0.0)
    m_out = lax.broadcasted_iota(jnp.int32, (4 * per, nrad * cdev), 0) // per
    m_in = (lax.broadcasted_iota(jnp.int32, (4 * per, nrad * cdev), 1) % cdev) // band_r
    built = jnp.zeros((4 * per, nrad * cdev), jnp.float32)
    for h in range(2):
        for p in range(2):
            part = jnp.dot(
                jnp.dot(
                    r_sel, radial_ref[p, h], precision=HIGHEST, preferred_element_type=jnp.float32
                ),
                c_sel,
                precision=HIGHEST,
                preferred_element_type=jnp.float32,
            )
            if p == 0:
                built = jnp.where((m_out == m_in) & (m_out % 2 == h), part, built)
            else:
                built = jnp.where((m_out == h) & (m_in == 2 + h), -part, built)
                built = jnp.where((m_out == 2 + h) & (m_in == h), part, built)
    radmat[...] = built

    def mix_and_send(k):
        total = one_s[k]
        for d in range(1, nax):
            gather_one(k, d).wait_recv()
        for d in range(1, nax):
            total = total + one_r[k, lax.rem(j + d, nax)]
        outs = []
        for h in range(2):
            prod = lax.dot_general(
                total,
                axmat[h],
                (((1,), (1,)), ((), ())),
                precision=HIGHEST,
                preferred_element_type=jnp.float32,
            )
            a = prod[:, 0:lanes]
            b = prod[:, lanes : 2 * lanes]
            e = prod[:, 2 * lanes : 3 * lanes]
            f = pltpu.roll(e, half, 1)
            swap_b = pltpu.roll(b, rows // 2, 0)
            swap_f = pltpu.roll(f, rows // 2, 0)
            low = row < rows // 2
            outs.append(
                (jnp.where(low, a - swap_b, a + swap_b), jnp.where(low, e - swap_f, e + swap_f))
            )
        odd = (row // band_r) % 2 == 1
        two_r[k, i, :, 0:lanes] = jnp.where(odd, outs[1][0], outs[0][0])
        two_r[k, i, :, lanes : 2 * lanes] = jnp.where(odd, outs[1][1], outs[0][1])
        for d in range(1, nrad):
            gather_two(k, d).start()

    def finish_coarse(k):
        for d in range(1, nrad):
            gather_two(k, d).wait_recv()
        return jnp.dot(
            radmat[...],
            two_r[k].reshape(nrad * cdev, 2 * lanes),
            precision=HIGHEST,
            preferred_element_type=jnp.float32,
        )

    mix_and_send(0)
    on_faces(lambda d: stiff_copy(d ^ 1).wait_recv())

    mass = [mass_ref[0], mass_ref[1]]

    def around(value, up, dn, lo, hi, t):
        return (
            jnp.where(row == 0, up, pltpu.roll(value, 1, 0)),
            jnp.where(row == rows - 1, dn, pltpu.roll(value, rows - 1, 0)),
            jnp.where(lane == 0, pltpu.roll(lo, lax.rem(lanes - t, lanes), 1), pltpu.roll(value, 1, 1)),
            jnp.where(lane == lanes - 1, pltpu.roll(hi, lanes - 1 - t, 1), pltpu.roll(value, lanes - 1, 1)),
        )

    def put_halo(k, t, y, packs):
        out = []
        for c in range(4):
            row_s[k, 0, c, pl.ds(t, 1), :] = y[c][0:1]
            row_s[k, 1, c, pl.ds(t, 1), :] = y[c][rows - 1 : rows]
            out.extend(pack(y[c], t, packs[2 * c], packs[2 * c + 1]))
        return tuple(out)

    def smooth(t, rr, ri, h):
        d_re, d_im, scale = dr[h, t], di[t], sc[h, t]
        return (d_re * rr + d_im * ri) * scale, (d_re * ri - d_im * rr) * scale

    def setup_pass(t, packs):
        value = stiff[t + 1]
        up, dn, lo, hi = around(
            value,
            srow_r[0, pl.ds(t, 1), :],
            srow_r[1, pl.ds(t, 1), :],
            scol_r[0],
            scol_r[1],
            t,
        )
        c_up, c_dn = 0.5 * (value + up), 0.5 * (value + dn)
        c_lo, c_hi = 0.5 * (value + lo), 0.5 * (value + hi)
        c_be, c_ah = 0.5 * (value + stiff[t]), 0.5 * (value + stiff[t + 2])
        wr_up[t] = c_up
        wr_dn[t] = c_dn
        wa_lo[t] = c_lo
        wa_hi[t] = c_hi
        wt[t] = c_be
        wt[t + 1] = c_ah
        total = c_dn + c_up + c_hi + c_lo + c_ah + c_be
        density = lookup(ids_ref[t], dens_ref)
        d_im = LOSS_FACTOR * total
        di[t] = d_im
        y = [None] * 4
        for h in range(2):
            d_re = total - mass[h] * density
            scale = RELAXATION / (d_re * d_re + d_im * d_im)
            dr[h, t] = d_re
            sc[h, t] = scale
            rr, ri = rhs_ref[0, h, t], rhs_ref[1, h, t]
            y[h] = (d_re * rr + d_im * ri) * scale
            y[2 + h] = (d_re * ri - d_im * rr) * scale
            sol_ref[0, h, t] = y[h]
            sol_ref[1, h, t] = y[2 + h]
        return put_halo(0, t, y, packs)

    def send_halo(k, packs):
        for c in range(4):
            col_s[k, 0, c] = packs[2 * c]
            col_s[k, 1, c] = packs[2 * c + 1]
        on_faces(lambda d: halo_copy(k, d).start())

    send_halo(0, lax.fori_loop(0, ct, setup_pass, (zero,) * 8))

    cosines, sines = [], []
    for h in range(2):
        angle = jnp.full((rows, lanes), harm_ref[h], jnp.int32).astype(jnp.float32) * (
            2.0 * jnp.pi / NSECT
        )
        cosines.append(jnp.cos(angle))
        sines.append(jnp.sin(angle))

    for k in range(ITERS):
        final = k == ITERS - 1
        coarse = finish_coarse(k)
        corr = [coarse[c * per : c * per + rows, 0:lanes] for c in range(4)]
        on_faces(lambda d: halo_copy(k, d ^ 1).wait_recv())
        cols = []
        for c in range(4):
            for s in range(2):
                at = c * per + rows + s
                row_r[k, s, c] = row_r[k, s, c] + coarse[at : at + 1, 0:lanes]
                cols.append(
                    col_r[k, s, c]
                    + coarse[c * per : c * per + rows, lanes + s : lanes + s + 1]
                )
        for c in range(4):
            col_r[k, 0, c] = cols[2 * c]
            col_r[k, 1, c] = cols[2 * c + 1]

        def load(t):
            return [sol_ref[c // 2, c % 2, t] + corr[c] for c in range(4)]

        def turn(x, sign):
            return [cosines[h] * x[h] - sign * sines[h] * x[2 + h] for h in range(2)] + [
                sign * sines[h] * x[h] + cosines[h] * x[2 + h] for h in range(2)
            ]

        start = load(0)
        beyond = turn(start, 1.0)
        before = turn(load(ct - 1), -1.0)

        def stencil(t, xm, x, xp):
            c_up, c_dn, c_lo, c_hi = wr_up[t], wr_dn[t], wa_lo[t], wa_hi[t]
            c_be, c_ah = wt[t], wt[t + 1]
            nb = []
            for c in range(4):
                up, dn, lo, hi = around(
                    x[c],
                    row_r[k, 0, c, pl.ds(t, 1), :],
                    row_r[k, 1, c, pl.ds(t, 1), :],
                    col_r[k, 0, c],
                    col_r[k, 1, c],
                    t,
                )
                nb.append(
                    (c_dn * dn + c_up * up)
                    + (c_hi * hi + c_lo * lo)
                    + (c_ah * xp[c] + c_be * xm[c])
                )
            d_im = di[t]
            res = [None] * 4
            for h in range(2):
                d_re = dr[h, t]
                re, im = h, 2 + h
                res[re] = rhs_ref[0, h, t] - (
                    d_re * x[re] - d_im * x[im] - (nb[re] - LOSS_FACTOR * nb[im])
                )
                res[im] = rhs_ref[1, h, t] - (
                    d_re * x[im] + d_im * x[re] - (nb[im] + LOSS_FACTOR * nb[re])
                )
            return res

        def step(t, xm, x, xp, state):
            res = stencil(t, xm, x, xp)
            if final:
                for c in range(4):
                    sol_ref[c // 2, c % 2, t] = x[c]
                    res_ref[c // 2, c % 2, t] = res[c]
                return state
            y = [None] * 4
            for h in range(2):
                a, b = smooth(t, res[h], res[2 + h], h)
                y[h], y[2 + h] = x[h] + a, x[2 + h] + b
            for c in range(4):
                sol_ref[c // 2, c % 2, t] = y[c]
            sums = tuple(state[c] + res[c] for c in range(4))
            return sums + put_halo(k + 1, t, y, state[4:])

        def body(t, carry):
            xm, x, state = carry[0:4], carry[4:8], carry[8:]
            xp = tuple(load(t + 1))
            return tuple(x) + xp + tuple(step(t, xm, x, xp, state))

        state = () if final else (zero,) * 12
        carry = lax.fori_loop(0, ct - 1, body, tuple(before) + tuple(start) + state)
        state = step(ct - 1, carry[0:4], carry[4:8], beyond, carry[8:])
        if not final:
            restrict_and_send(k + 1, state[0:4])
            send_halo(k + 1, state[4:])
            mix_and_send(k + 1)

    on_faces(lambda d: stiff_copy(d).wait_send())
    for k in range(ITERS):
        on_faces(lambda d: halo_copy(k, d).wait_send())
        for d in range(1, nax):
            gather_one(k, d).wait_send()
        for d in range(1, nrad):
            gather_two(k, d).wait_send()


def local(rhs, mat_ids, stiff_table, dens_table, mass_shift, harmonic, radial_factor, axial_factor):
    nrad = lax.axis_size("radial")
    nax = lax.axis_size("axial")
    ct, rows, lanes = mat_ids.shape
    vmem = pl.BlockSpec(memory_space=pltpu.VMEM)
    smem = pl.BlockSpec(memory_space=pltpu.SMEM)
    f32 = jnp.float32
    field = (ct, rows, lanes)
    cdev = 4 * (rows // AR)
    dma = pltpu.SemaphoreType.DMA
    return pl.pallas_call(
        functools.partial(kernel, nrad, nax),
        out_shape=(jax.ShapeDtypeStruct(rhs.shape, f32), jax.ShapeDtypeStruct(rhs.shape, f32)),
        in_specs=[vmem, vmem, smem, smem, smem, smem, vmem, vmem],
        out_specs=(vmem, vmem),
        scratch_shapes=[
            pltpu.VMEM((ct + 2, rows, lanes), f32),
            pltpu.VMEM(field, f32),
            pltpu.VMEM(field, f32),
            pltpu.VMEM(field, f32),
            pltpu.VMEM(field, f32),
            pltpu.VMEM((ct + 1, rows, lanes), f32),
            pltpu.VMEM((2,) + field, f32),
            pltpu.VMEM(field, f32),
            pltpu.VMEM((2,) + field, f32),
            pltpu.VMEM((2, ct, lanes), f32),
            pltpu.VMEM((2, ct, lanes), f32),
            pltpu.VMEM((2, rows, lanes), f32),
            pltpu.VMEM((2, rows, lanes), f32),
            pltpu.VMEM((ITERS, 2, 4, ct, lanes), f32),
            pltpu.VMEM((ITERS, 2, 4, ct, lanes), f32),
            pltpu.VMEM((ITERS, 2, 4, rows, lanes), f32),
            pltpu.VMEM((ITERS, 2, 4, rows, lanes), f32),
            pltpu.VMEM((ITERS, rows, lanes), f32),
            pltpu.VMEM((ITERS, nax, rows, lanes), f32),
            pltpu.VMEM((ITERS, nrad, rows, 2 * lanes), f32),
            pltpu.VMEM((2, 3 * lanes, lanes), f32),
            pltpu.VMEM((8 * rows, nrad * cdev), f32),
            dma((4,)),
            dma((4,)),
            dma((ITERS, 4)),
            dma((ITERS, 4)),
            dma((ITERS, nax)),
            dma((ITERS, nax)),
            dma((ITERS, nrad)),
            dma((ITERS, nrad)),
        ],
        compiler_params=pltpu.CompilerParams(
            collective_id=0, has_side_effects=True, vmem_limit_bytes=40 * 1024 * 1024
        ),
    )(rhs, mat_ids, stiff_table, dens_table, mass_shift, harmonic, radial_factor, axial_factor)


def solution(mesh):
    return jax.shard_map(
        local,
        mesh=mesh,
        in_specs=(
            P(None, None, None, "radial", "axial"),
            P(None, "radial", "axial"),
            P(),
            P(),
            P(),
            P(),
            P(),
            P(),
        ),
        out_specs=(P(None, None, None, "radial", "axial"), P(None, None, None, "radial", "axial")),
        check_vma=False,
    )
```

```python
import functools

import jax
import jax.numpy as jnp
from jax import lax
from jax.experimental import pallas as pl
from jax.experimental.pallas import tpu as pltpu
from jax.sharding import PartitionSpec as P

ITERS = 3
NSECT = 24
AR = 4
AA = 8
LOSS_FACTOR = 0.2
RELAXATION = 0.6
MESH = pl.DeviceIdType.MESH
HIGHEST = lax.Precision.HIGHEST
CHUNK = 8


def kernel(
    nrad,
    nax,
    rhs_hbm,
    ids_hbm,
    stiff_hbm,
    dens_hbm,
    mass_hbm,
    harm_hbm,
    radial_hbm,
    axial_hbm,
    sol_ref,
    res_ref,
    rhs_ref,
    ids_ref,
    stiff_ref,
    dens_ref,
    mass_ref,
    harm_ref,
    radial_ref,
    axial_ref,
    in_sem,
    stiff,
    wr_up,
    wr_dn,
    wa_lo,
    wa_hi,
    wt,
    dr,
    di,
    sc,
    srow_s,
    srow_r,
    scol_s,
    scol_r,
    row_s,
    row_r,
    col_s,
    col_r,
    col_m,
    one_s,
    one_r,
    two_r,
    axmat,
    radmat,
    st_send,
    st_recv,
    ha_send,
    ha_recv,
    g1_send,
    g1_recv,
    g2_send,
    g2_recv,
):
    loads = [
        pltpu.make_async_copy(src, dst, in_sem.at[n])
        for n, (src, dst) in enumerate(
            (
                (stiff_hbm, stiff_ref),
                (ids_hbm, ids_ref),
                (rhs_hbm, rhs_ref),
                (dens_hbm, dens_ref),
                (mass_hbm, mass_ref),
                (harm_hbm, harm_ref),
                (radial_hbm, radial_ref),
                (axial_hbm, axial_ref),
            )
        )
    ]
    for load_in in loads:
        load_in.start()
    ct = rhs_ref.shape[2]
    rows, lanes = rhs_ref.shape[3:]
    gr = radial_ref.shape[2]
    ga = axial_ref.shape[2]
    band_r = rows // AR
    band_c = lanes // AA
    i = lax.axis_index("radial")
    j = lax.axis_index("axial")
    has_up, has_dn = i > 0, i < nrad - 1
    has_lo, has_hi = j > 0, j < nax - 1
    conds = (has_up, has_dn, has_lo, has_hi)
    targets = ({"radial": i - 1}, {"radial": i + 1}, {"axial": j - 1}, {"axial": j + 1})

    for d in range(4):

        @pl.when(jnp.logical_not(conds[d]))
        def _():
            if d < 2:
                srow_r[d] = jnp.zeros(srow_r.shape[1:], jnp.float32)
                for k in range(ITERS):
                    row_r[k, d] = jnp.zeros(row_r.shape[2:], jnp.float32)
            else:
                scol_r[d - 2] = jnp.zeros(scol_r.shape[1:], jnp.float32)
                for k in range(ITERS):
                    col_r[k, d - 2] = jnp.zeros(col_r.shape[2:], jnp.float32)

    barrier = pltpu.get_barrier_semaphore()
    for d in range(1, nax):
        pl.semaphore_signal(
            barrier, inc=1, device_id={"axial": lax.rem(j + d, nax)}, device_id_type=MESH
        )
    for d in range(1, nrad):
        pl.semaphore_signal(
            barrier, inc=1, device_id={"radial": lax.rem(i + d, nrad)}, device_id_type=MESH
        )

    row = lax.broadcasted_iota(jnp.int32, (rows, lanes), 0)
    lane = lax.broadcasted_iota(jnp.int32, (rows, lanes), 1)
    zero = jnp.zeros((rows, lanes), jnp.float32)

    def lookup(ids, table):
        value = jnp.full(ids.shape, table[0], jnp.float32)
        for entry in range(1, table.shape[0]):
            value = jnp.where(ids == entry, table[entry], value)
        return value

    cap = lanes // 2
    pair = lane // 2

    def pack(value, t, packed):
        at = lax.rem(t, cap)
        return jnp.where(pair == at, pltpu.roll(value, 2 * at + 1, 1), packed)

    def stiff_copy(d):
        if d < 2:
            src, dst = srow_s.at[d], srow_r.at[1 - d]
        else:
            src, dst = scol_s, scol_r.at[3 - d]
        return pltpu.make_async_remote_copy(
            src_ref=src,
            dst_ref=dst,
            send_sem=st_send.at[d],
            recv_sem=st_recv.at[d ^ 1],
            device_id=targets[d],
            device_id_type=MESH,
        )

    def halo_copy(k, d):
        if d < 2:
            src, dst = row_s.at[k, d], row_r.at[k, 1 - d]
        else:
            src, dst = col_s.at[k], col_r.at[k, 3 - d]
        return pltpu.make_async_remote_copy(
            src_ref=src,
            dst_ref=dst,
            send_sem=ha_send.at[k, d],
            recv_sem=ha_recv.at[k, d ^ 1],
            device_id=targets[d],
            device_id_type=MESH,
        )

    def gather_one(k, d):
        return pltpu.make_async_remote_copy(
            src_ref=one_s.at[k],
            dst_ref=one_r.at[k, j],
            send_sem=g1_send.at[k, d],
            recv_sem=g1_recv.at[k, d],
            device_id={"axial": lax.rem(j + d, nax)},
            device_id_type=MESH,
        )

    def gather_two(k, d):
        return pltpu.make_async_remote_copy(
            src_ref=two_r.at[k, i],
            dst_ref=two_r.at[k, i],
            send_sem=g2_send.at[k, d],
            recv_sem=g2_recv.at[k, d],
            device_id={"radial": lax.rem(i + d, nrad)},
            device_id_type=MESH,
        )

    def on_faces(act):
        for d in range(4):

            @pl.when(conds[d])
            def _():
                act(d)

    scol_s[...] = jnp.zeros(scol_s.shape, jnp.float32)
    col_s[...] = jnp.zeros(col_s.shape, jnp.float32)
    loads[0].wait()
    loads[1].wait()

    @pl.loop(0, ct // CHUNK)
    def _(chunk):
        begin = chunk * CHUNK
        tile = begin // cap
        packed = scol_s[tile]
        for u in range(CHUNK):
            t = begin + u
            value = lookup(ids_ref[t], stiff_ref)
            stiff[t + 1] = value
            srow_s[0, pl.ds(t, 1), :] = value[0:1]
            srow_s[1, pl.ds(t, 1), :] = value[rows - 1 : rows]
            packed = pack(value, t, packed)
        scol_s[tile] = packed

    stiff[0] = stiff[ct]
    stiff[ct + 1] = stiff[1]

    pl.semaphore_wait(barrier, nax + nrad - 2)
    on_faces(lambda d: stiff_copy(d).start())

    e_row = lax.broadcasted_iota(jnp.int32, (lanes, lanes), 0)
    e_col = lax.broadcasted_iota(jnp.int32, (lanes, lanes), 1)
    fold = jnp.where(e_row // AA + j * band_c == e_col, 1.0, 0.0)

    def restrict_and_send(k, sums):
        tile = zero
        for c in range(4):
            s = sums[c] + pltpu.roll(sums[c], rows - 1, 0)
            s = s + pltpu.roll(s, rows - 2, 0)
            for g in range(band_r):
                to = c * band_r + g
                moved = pltpu.roll(s, (to - g * AR) % rows, 0)
                tile = jnp.where(row == to, moved, tile)
        one_s[k] = jnp.dot(tile, fold, precision=HIGHEST, preferred_element_type=jnp.float32)
        for d in range(1, nax):
            gather_one(k, d).start()

    loads[2].wait()

    def sum_pass(chunk, sums):
        sums = list(sums)
        for u in range(CHUNK):
            for c in range(4):
                sums[c] = sums[c] + rhs_ref[c // 2, c % 2, chunk * CHUNK + u]
        return tuple(sums)

    restrict_and_send(0, lax.fori_loop(0, ct // CHUNK, sum_pass, (zero,) * 4))
    for load_in in loads[3:]:
        load_in.wait()

    ax_row = lax.broadcasted_iota(jnp.int32, (lanes, ga), 0)
    ax_col = lax.broadcasted_iota(jnp.int32, (lanes, ga), 1)
    own = jnp.where(ax_row // AA + j * band_c == ax_col, 1.0, 0.0)
    edge_lo = j * band_c - 1
    edge_hi = (j + 1) * band_c
    half = lanes // 2
    edges = []
    for p in range(2):
        hit = ((ax_row == p * half) & (ax_col == edge_lo)) | (
            (ax_row == p * half + 1) & (ax_col == edge_hi)
        )
        edges.append(jnp.where(hit, 1.0, 0.0))
    for h in range(2):
        if ga < lanes:
            axmat[h] = jnp.zeros(axmat.shape[1:], jnp.float32)

        def spread(select, p):
            return jnp.dot(
                select, axial_ref[p, h], precision=HIGHEST, preferred_element_type=jnp.float32
            )

        axmat[h, 0:lanes, 0:ga] = spread(own, 0)
        axmat[h, lanes : 2 * lanes, 0:ga] = spread(own, 1)
        axmat[h, 2 * lanes : 3 * lanes, 0:ga] = spread(edges[0], 0) + spread(edges[1], 1)

    per = 2 * rows
    cdev = 4 * band_r
    r_row = lax.broadcasted_iota(jnp.int32, (4 * per, gr), 0) % per
    r_col = lax.broadcasted_iota(jnp.int32, (4 * per, gr), 1)
    want = jnp.where(
        r_row < rows,
        r_row // AR + i * band_r,
        jnp.where(
            r_row == rows, i * band_r - 1, jnp.where(r_row == rows + 1, (i + 1) * band_r, -1)
        ),
    )
    r_sel = jnp.where(want == r_col, 1.0, 0.0)
    c_row = lax.broadcasted_iota(jnp.int32, (gr, nrad * cdev), 0)
    c_col = lax.broadcasted_iota(jnp.int32, (gr, nrad * cdev), 1)
    c_sel = jnp.where((c_col // cdev) * band_r + c_col % band_r == c_row, 1.0, 0.0)
    m_out = lax.broadcasted_iota(jnp.int32, (4 * per, nrad * cdev), 0) // per
    m_in = (lax.broadcasted_iota(jnp.int32, (4 * per, nrad * cdev), 1) % cdev) // band_r
    built = jnp.zeros((4 * per, nrad * cdev), jnp.float32)
    for h in range(2):
        for p in range(2):
            part = jnp.dot(
                jnp.dot(
                    r_sel, radial_ref[p, h], precision=HIGHEST, preferred_element_type=jnp.float32
                ),
                c_sel,
                precision=HIGHEST,
                preferred_element_type=jnp.float32,
            )
            if p == 0:
                built = jnp.where((m_out == m_in) & (m_out % 2 == h), part, built)
            else:
                built = jnp.where((m_out == h) & (m_in == 2 + h), -part, built)
                built = jnp.where((m_out == 2 + h) & (m_in == h), part, built)
    radmat[...] = built

    def mix_and_send(k):
        total = one_s[k]
        for d in range(1, nax):
            gather_one(k, d).wait_recv()
        for d in range(1, nax):
            total = total + one_r[k, lax.rem(j + d, nax)]
        outs = []
        for h in range(2):
            prod = lax.dot_general(
                total,
                axmat[h],
                (((1,), (1,)), ((), ())),
                precision=HIGHEST,
                preferred_element_type=jnp.float32,
            )
            a = prod[:, 0:lanes]
            b = prod[:, lanes : 2 * lanes]
            e = prod[:, 2 * lanes : 3 * lanes]
            f = pltpu.roll(e, half, 1)
            swap_b = pltpu.roll(b, rows // 2, 0)
            swap_f = pltpu.roll(f, rows // 2, 0)
            low = row < rows // 2
            outs.append(
                (jnp.where(low, a - swap_b, a + swap_b), jnp.where(low, e - swap_f, e + swap_f))
            )
        odd = (row // band_r) % 2 == 1
        two_r[k, i, :, 0:lanes] = jnp.where(odd, outs[1][0], outs[0][0])
        two_r[k, i, :, lanes : 2 * lanes] = jnp.where(odd, outs[1][1], outs[0][1])
        for d in range(1, nrad):
            gather_two(k, d).start()

    def finish_coarse(k):
        for d in range(1, nrad):
            gather_two(k, d).wait_recv()
        return jnp.dot(
            radmat[...],
            two_r[k].reshape(nrad * cdev, 2 * lanes),
            precision=HIGHEST,
            preferred_element_type=jnp.float32,
        )

    mix_and_send(0)
    on_faces(lambda d: stiff_copy(d ^ 1).wait_recv())

    mass = [mass_ref[0], mass_ref[1]]

    odd_lane = lane % 2 == 1

    def around(value, up, dn, beside, t):
        edge = pltpu.roll(beside, lanes - 1 - 2 * lax.rem(t, cap), 1)
        return (
            jnp.where(row == 0, up, pltpu.roll(value, 1, 0)),
            jnp.where(row == rows - 1, dn, pltpu.roll(value, rows - 1, 0)),
            pltpu.roll(jnp.where(lane == lanes - 1, edge, value), 1, 1),
            pltpu.roll(jnp.where(lane == 0, edge, value), lanes - 1, 1),
        )

    def put_rows(k, t, y):
        for c in range(4):
            row_s[k, 0, c, pl.ds(t, 1), :] = y[c][0:1]
            row_s[k, 1, c, pl.ds(t, 1), :] = y[c][rows - 1 : rows]

    def smooth(t, rr, ri, h):
        d_re, d_im, scale = dr[h, t], di[t], sc[h, t]
        return (d_re * rr + d_im * ri) * scale, (d_re * ri - d_im * rr) * scale

    for n in range(scol_s.shape[0]):
        col_m[0, n] = jnp.where(odd_lane, scol_r[1, n], scol_r[0, n])

    def setup_step(t, packs, beside):
        value = stiff[t + 1]
        up, dn, lo, hi = around(
            value,
            srow_r[0, pl.ds(t, 1), :],
            srow_r[1, pl.ds(t, 1), :],
            beside,
            t,
        )
        c_up, c_dn = 0.5 * (value + up), 0.5 * (value + dn)
        c_lo, c_hi = 0.5 * (value + lo), 0.5 * (value + hi)
        c_be, c_ah = 0.5 * (value + stiff[t]), 0.5 * (value + stiff[t + 2])
        wr_up[t] = c_up
        wr_dn[t] = c_dn
        wa_lo[t] = c_lo
        wa_hi[t] = c_hi
        wt[t] = c_be
        wt[t + 1] = c_ah
        total = c_dn + c_up + c_hi + c_lo + c_ah + c_be
        density = lookup(ids_ref[t], dens_ref)
        d_im = LOSS_FACTOR * total
        di[t] = d_im
        y = [None] * 4
        for h in range(2):
            d_re = total - mass[h] * density
            scale = RELAXATION / (d_re * d_re + d_im * d_im)
            dr[h, t] = d_re
            sc[h, t] = scale
            rr, ri = rhs_ref[0, h, t], rhs_ref[1, h, t]
            y[h] = (d_re * rr + d_im * ri) * scale
            y[2 + h] = (d_re * ri - d_im * rr) * scale
            sol_ref[0, h, t] = y[h]
            sol_ref[1, h, t] = y[2 + h]
        put_rows(0, t, y)
        return [pack(y[c], t, packs[c]) for c in range(4)]

    @pl.loop(0, ct // CHUNK)
    def _(chunk):
        begin = chunk * CHUNK
        tile = begin // cap
        beside = col_m[0, tile]
        packs = [col_s[0, c, tile] for c in range(4)]
        for u in range(CHUNK):
            packs = setup_step(begin + u, packs, beside)
        for c in range(4):
            col_s[0, c, tile] = packs[c]

    on_faces(lambda d: halo_copy(0, d).start())

    cosines, sines = [], []
    for h in range(2):
        angle = jnp.full((rows, lanes), harm_ref[h], jnp.int32).astype(jnp.float32) * (
            2.0 * jnp.pi / NSECT
        )
        cosines.append(jnp.cos(angle))
        sines.append(jnp.sin(angle))

    for k in range(ITERS):
        final = k == ITERS - 1
        coarse = finish_coarse(k)
        corr = [coarse[c * per : c * per + rows, 0:lanes] for c in range(4)]
        on_faces(lambda d: halo_copy(k, d ^ 1).wait_recv())
        for c in range(4):
            add = []
            for side in range(2):
                at = c * per + rows + side
                row_r[k, side, c] = row_r[k, side, c] + coarse[at : at + 1, 0:lanes]
                add.append(coarse[c * per : c * per + rows, lanes + side : lanes + side + 1])
            for n in range(col_m.shape[1]):
                col_m[c, n] = jnp.where(
                    odd_lane, col_r[k, 1, c, n] + add[1], col_r[k, 0, c, n] + add[0]
                )

        def load(t):
            return [sol_ref[c // 2, c % 2, t] + corr[c] for c in range(4)]

        def turn(x, sign):
            return [cosines[h] * x[h] - sign * sines[h] * x[2 + h] for h in range(2)] + [
                sign * sines[h] * x[h] + cosines[h] * x[2 + h] for h in range(2)
            ]

        start = load(0)
        beyond = turn(start, 1.0)
        before = turn(load(ct - 1), -1.0)

        def stencil(t, xm, x, xp, beside):
            c_up, c_dn, c_lo, c_hi = wr_up[t], wr_dn[t], wa_lo[t], wa_hi[t]
            c_be, c_ah = wt[t], wt[t + 1]
            nb = []
            for c in range(4):
                up, dn, lo, hi = around(
                    x[c],
                    row_r[k, 0, c, pl.ds(t, 1), :],
                    row_r[k, 1, c, pl.ds(t, 1), :],
                    beside[c],
                    t,
                )
                nb.append(
                    (c_dn * dn + c_up * up)
                    + (c_hi * hi + c_lo * lo)
                    + (c_ah * xp[c] + c_be * xm[c])
                )
            d_im = di[t]
            res = [None] * 4
            for h in range(2):
                d_re = dr[h, t]
                re, im = h, 2 + h
                res[re] = rhs_ref[0, h, t] - (
                    d_re * x[re] - d_im * x[im] - (nb[re] - LOSS_FACTOR * nb[im])
                )
                res[im] = rhs_ref[1, h, t] - (
                    d_re * x[im] + d_im * x[re] - (nb[im] + LOSS_FACTOR * nb[re])
                )
            return res

        def chunk_pass(chunk, carry):
            xm, x, sums = list(carry[0:4]), list(carry[4:8]), list(carry[8:])
            begin = chunk * CHUNK
            tile = begin // cap
            beside = [col_m[c, tile] for c in range(4)]
            if not final:
                packs = [col_s[k + 1, c, tile] for c in range(4)]
            for u in range(CHUNK):
                t = begin + u
                if u < CHUNK - 1:
                    xp = load(t + 1)
                else:
                    ended = t == ct - 1
                    xp = load(jnp.minimum(t + 1, ct - 1))
                    xp = [jnp.where(ended, beyond[c], xp[c]) for c in range(4)]
                res = stencil(t, xm, x, xp, beside)
                if final:
                    for c in range(4):
                        sol_ref[c // 2, c % 2, t] = x[c]
                        res_ref[c // 2, c % 2, t] = res[c]
                else:
                    y = [None] * 4
                    for h in range(2):
                        a, b = smooth(t, res[h], res[2 + h], h)
                        y[h], y[2 + h] = x[h] + a, x[2 + h] + b
                    for c in range(4):
                        sol_ref[c // 2, c % 2, t] = y[c]
                        sums[c] = sums[c] + res[c]
                        packs[c] = pack(y[c], t, packs[c])
                    put_rows(k + 1, t, y)
                xm, x = x, xp
            if not final:
                for c in range(4):
                    col_s[k + 1, c, tile] = packs[c]
            return tuple(xm) + tuple(x) + tuple(sums)

        state = () if final else (zero,) * 4
        carry = lax.fori_loop(0, ct // CHUNK, chunk_pass, tuple(before) + tuple(start) + state)
        if not final:
            restrict_and_send(k + 1, carry[8:])
            on_faces(lambda d: halo_copy(k + 1, d).start())
            mix_and_send(k + 1)

    on_faces(lambda d: stiff_copy(d).wait_send())
    for k in range(ITERS):
        on_faces(lambda d: halo_copy(k, d).wait_send())
        for d in range(1, nax):
            gather_one(k, d).wait_send()
        for d in range(1, nrad):
            gather_two(k, d).wait_send()


def local(rhs, mat_ids, stiff_table, dens_table, mass_shift, harmonic, radial_factor, axial_factor):
    nrad = lax.axis_size("radial")
    nax = lax.axis_size("axial")
    ct, rows, lanes = mat_ids.shape
    vmem = pl.BlockSpec(memory_space=pltpu.VMEM)
    hbm = pl.BlockSpec(memory_space=pltpu.HBM)
    tiles = -(-2 * ct // lanes)
    f32 = jnp.float32
    field = (ct, rows, lanes)
    cdev = 4 * (rows // AR)
    dma = pltpu.SemaphoreType.DMA
    return pl.pallas_call(
        functools.partial(kernel, nrad, nax),
        out_shape=(jax.ShapeDtypeStruct(rhs.shape, f32), jax.ShapeDtypeStruct(rhs.shape, f32)),
        in_specs=[hbm] * 8,
        out_specs=(vmem, vmem),
        scratch_shapes=[
            pltpu.VMEM(rhs.shape, f32),
            pltpu.VMEM(field, jnp.int32),
            pltpu.SMEM(stiff_table.shape, f32),
            pltpu.SMEM(dens_table.shape, f32),
            pltpu.SMEM(mass_shift.shape, f32),
            pltpu.SMEM(harmonic.shape, jnp.int32),
            pltpu.VMEM(radial_factor.shape, f32),
            pltpu.VMEM(axial_factor.shape, f32),
            dma((8,)),
            pltpu.VMEM((ct + 2, rows, lanes), f32),
            pltpu.VMEM(field, f32),
            pltpu.VMEM(field, f32),
            pltpu.VMEM(field, f32),
            pltpu.VMEM(field, f32),
            pltpu.VMEM((ct + 1, rows, lanes), f32),
            pltpu.VMEM((2,) + field, f32),
            pltpu.VMEM(field, f32),
            pltpu.VMEM((2,) + field, f32),
            pltpu.VMEM((2, ct, lanes), f32),
            pltpu.VMEM((2, ct, lanes), f32),
            pltpu.VMEM((tiles, rows, lanes), f32),
            pltpu.VMEM((2, tiles, rows, lanes), f32),
            pltpu.VMEM((ITERS, 2, 4, ct, lanes), f32),
            pltpu.VMEM((ITERS, 2, 4, ct, lanes), f32),
            pltpu.VMEM((ITERS, 4, tiles, rows, lanes), f32),
            pltpu.VMEM((ITERS, 2, 4, tiles, rows, lanes), f32),
            pltpu.VMEM((4, tiles, rows, lanes), f32),
            pltpu.VMEM((ITERS, rows, lanes), f32),
            pltpu.VMEM((ITERS, nax, rows, lanes), f32),
            pltpu.VMEM((ITERS, nrad, rows, 2 * lanes), f32),
            pltpu.VMEM((2, 3 * lanes, lanes), f32),
            pltpu.VMEM((8 * rows, nrad * cdev), f32),
            dma((4,)),
            dma((4,)),
            dma((ITERS, 4)),
            dma((ITERS, 4)),
            dma((ITERS, nax)),
            dma((ITERS, nax)),
            dma((ITERS, nrad)),
            dma((ITERS, nrad)),
        ],
        compiler_params=pltpu.CompilerParams(
            collective_id=0, has_side_effects=True, vmem_limit_bytes=58 * 1024 * 1024
        ),
    )(rhs, mat_ids, stiff_table, dens_table, mass_shift, harmonic, radial_factor, axial_factor)


def solution(mesh):
    return jax.shard_map(
        local,
        mesh=mesh,
        in_specs=(
            P(None, None, None, "radial", "axial"),
            P(None, "radial", "axial"),
            P(),
            P(),
            P(),
            P(),
            P(),
            P(),
        ),
        out_specs=(P(None, None, None, "radial", "axial"), P(None, None, None, "radial", "axial")),
        check_vma=False,
    )
```

```python
import functools

import jax
import jax.numpy as jnp
from jax import lax
from jax.experimental import pallas as pl
from jax.experimental.pallas import tpu as pltpu
from jax.sharding import PartitionSpec as P

ITERS = 3
NSECT = 24
AR = 4
AA = 8
LOSS_FACTOR = 0.2
RELAXATION = 0.6
MESH = pl.DeviceIdType.MESH
HIGHEST = lax.Precision.HIGHEST
CHUNK = 8


def kernel(
    nrad,
    nax,
    rhs_hbm,
    ids_hbm,
    stiff_hbm,
    dens_hbm,
    mass_hbm,
    harm_hbm,
    radial_hbm,
    axial_hbm,
    sol_ref,
    res_ref,
    rhs_ref,
    ids_ref,
    stiff_ref,
    dens_ref,
    mass_ref,
    harm_ref,
    radial_ref,
    axial_ref,
    in_sem,
    stiff,
    wr_up,
    wr_dn,
    wa_lo,
    wa_hi,
    wt,
    dr,
    di,
    sc,
    srow_s,
    srow_r,
    scol_s,
    scol_r,
    row_s,
    row_r,
    col_s,
    col_r,
    col_m,
    one_s,
    one_r,
    two_r,
    axmat,
    radmat,
    st_send,
    st_recv,
    ha_send,
    ha_recv,
    g1_send,
    g1_recv,
    g2_send,
    g2_recv,
):
    loads = [
        pltpu.make_async_copy(src, dst, in_sem.at[n])
        for n, (src, dst) in enumerate(
            (
                (stiff_hbm, stiff_ref),
                (ids_hbm, ids_ref),
                (rhs_hbm, rhs_ref),
                (dens_hbm, dens_ref),
                (mass_hbm, mass_ref),
                (harm_hbm, harm_ref),
                (radial_hbm, radial_ref),
                (axial_hbm, axial_ref),
            )
        )
    ]
    for load_in in loads:
        load_in.start()
    ct = rhs_ref.shape[2]
    rows, lanes = rhs_ref.shape[3:]
    gr = radial_ref.shape[2]
    ga = axial_ref.shape[2]
    band_r = rows // AR
    band_c = lanes // AA
    i = lax.axis_index("radial")
    j = lax.axis_index("axial")
    has_up, has_dn = i > 0, i < nrad - 1
    has_lo, has_hi = j > 0, j < nax - 1
    conds = (has_up, has_dn, has_lo, has_hi)
    targets = ({"radial": i - 1}, {"radial": i + 1}, {"axial": j - 1}, {"axial": j + 1})

    for d in range(4):

        @pl.when(jnp.logical_not(conds[d]))
        def _():
            if d < 2:
                srow_r[d] = jnp.zeros(srow_r.shape[1:], jnp.float32)
                for k in range(ITERS):
                    row_r[k, d] = jnp.zeros(row_r.shape[2:], jnp.float32)
            else:
                scol_r[d - 2] = jnp.zeros(scol_r.shape[1:], jnp.float32)
                for k in range(ITERS):
                    col_r[k, d - 2] = jnp.zeros(col_r.shape[2:], jnp.float32)

    barrier = pltpu.get_barrier_semaphore()
    for d in range(1, nax):
        pl.semaphore_signal(
            barrier, inc=1, device_id={"axial": lax.rem(j + d, nax)}, device_id_type=MESH
        )
    for d in range(1, nrad):
        pl.semaphore_signal(
            barrier, inc=1, device_id={"radial": lax.rem(i + d, nrad)}, device_id_type=MESH
        )

    row = lax.broadcasted_iota(jnp.int32, (rows, lanes), 0)
    lane = lax.broadcasted_iota(jnp.int32, (rows, lanes), 1)
    zero = jnp.zeros((rows, lanes), jnp.float32)

    def lookup(ids, table):
        value = jnp.full(ids.shape, table[0], jnp.float32)
        for entry in range(1, table.shape[0]):
            value = jnp.where(ids == entry, table[entry], value)
        return value

    cap = lanes // 2
    pair = lane // 2

    def pack(value, t, packed):
        at = lax.rem(t, cap)
        return jnp.where(pair == at, pltpu.roll(value, 2 * at + 1, 1), packed)

    def stiff_copy(d):
        if d < 2:
            src, dst = srow_s.at[d], srow_r.at[1 - d]
        else:
            src, dst = scol_s, scol_r.at[3 - d]
        return pltpu.make_async_remote_copy(
            src_ref=src,
            dst_ref=dst,
            send_sem=st_send.at[d],
            recv_sem=st_recv.at[d ^ 1],
            device_id=targets[d],
            device_id_type=MESH,
        )

    middle = 3 * (ct // CHUNK) // 4

    def halo_copy(k, d, late=1):
        if d < 2:
            part = pl.ds(middle * CHUNK, ct - middle * CHUNK) if late else pl.ds(0, middle * CHUNK)
            src, dst = row_s.at[k, d, :, part], row_r.at[k, 1 - d, :, part]
        else:
            src, dst = col_s.at[k], col_r.at[k, 3 - d]
        return pltpu.make_async_remote_copy(
            src_ref=src,
            dst_ref=dst,
            send_sem=ha_send.at[k, late, d],
            recv_sem=ha_recv.at[k, late, d ^ 1],
            device_id=targets[d],
            device_id_type=MESH,
        )

    def gather_one(k, d):
        return pltpu.make_async_remote_copy(
            src_ref=one_s.at[k],
            dst_ref=one_r.at[k, j],
            send_sem=g1_send.at[k, d],
            recv_sem=g1_recv.at[k, d],
            device_id={"axial": lax.rem(j + d, nax)},
            device_id_type=MESH,
        )

    def gather_two(k, d):
        return pltpu.make_async_remote_copy(
            src_ref=two_r.at[k, i],
            dst_ref=two_r.at[k, i],
            send_sem=g2_send.at[k, d],
            recv_sem=g2_recv.at[k, d],
            device_id={"radial": lax.rem(i + d, nrad)},
            device_id_type=MESH,
        )

    def on_faces(act, faces=4):
        for d in range(faces):

            @pl.when(conds[d])
            def _():
                act(d)

    scol_s[...] = jnp.zeros(scol_s.shape, jnp.float32)
    col_s[...] = jnp.zeros(col_s.shape, jnp.float32)
    loads[0].wait()
    loads[1].wait()

    @pl.loop(0, ct // CHUNK)
    def _(chunk):
        begin = chunk * CHUNK
        tile = begin // cap
        packed = scol_s[tile]
        for u in range(CHUNK):
            t = begin + u
            value = lookup(ids_ref[t], stiff_ref)
            stiff[t + 1] = value
            srow_s[0, pl.ds(t, 1), :] = value[0:1]
            srow_s[1, pl.ds(t, 1), :] = value[rows - 1 : rows]
            packed = pack(value, t, packed)
        scol_s[tile] = packed

    stiff[0] = stiff[ct]
    stiff[ct + 1] = stiff[1]

    pl.semaphore_wait(barrier, nax + nrad - 2)
    on_faces(lambda d: stiff_copy(d).start())

    e_row = lax.broadcasted_iota(jnp.int32, (lanes, lanes), 0)
    e_col = lax.broadcasted_iota(jnp.int32, (lanes, lanes), 1)
    fold = jnp.where(e_row // AA + j * band_c == e_col, 1.0, 0.0)

    def restrict_and_send(k, sums):
        tile = zero
        for c in range(4):
            s = sums[c] + pltpu.roll(sums[c], rows - 1, 0)
            s = s + pltpu.roll(s, rows - 2, 0)
            for g in range(band_r):
                to = c * band_r + g
                moved = pltpu.roll(s, (to - g * AR) % rows, 0)
                tile = jnp.where(row == to, moved, tile)
        one_s[k] = jnp.dot(tile, fold, precision=HIGHEST, preferred_element_type=jnp.float32)
        for d in range(1, nax):
            gather_one(k, d).start()

    loads[2].wait()

    def sum_pass(chunk, sums):
        sums = list(sums)
        for u in range(CHUNK):
            for c in range(4):
                sums[c] = sums[c] + rhs_ref[c // 2, c % 2, chunk * CHUNK + u]
        return tuple(sums)

    restrict_and_send(0, lax.fori_loop(0, ct // CHUNK, sum_pass, (zero,) * 4))
    for load_in in loads[3:]:
        load_in.wait()

    ax_row = lax.broadcasted_iota(jnp.int32, (lanes, ga), 0)
    ax_col = lax.broadcasted_iota(jnp.int32, (lanes, ga), 1)
    own = jnp.where(ax_row // AA + j * band_c == ax_col, 1.0, 0.0)
    edge_lo = j * band_c - 1
    edge_hi = (j + 1) * band_c
    half = lanes // 2
    edges = []
    for p in range(2):
        hit = ((ax_row == p * half) & (ax_col == edge_lo)) | (
            (ax_row == p * half + 1) & (ax_col == edge_hi)
        )
        edges.append(jnp.where(hit, 1.0, 0.0))
    for h in range(2):
        if ga < lanes:
            axmat[h] = jnp.zeros(axmat.shape[1:], jnp.float32)

        def spread(select, p):
            return jnp.dot(
                select, axial_ref[p, h], precision=HIGHEST, preferred_element_type=jnp.float32
            )

        axmat[h, 0:lanes, 0:ga] = spread(own, 0)
        axmat[h, lanes : 2 * lanes, 0:ga] = spread(own, 1)
        axmat[h, 2 * lanes : 3 * lanes, 0:ga] = spread(edges[0], 0) + spread(edges[1], 1)

    per = 2 * rows
    cdev = 4 * band_r
    r_row = lax.broadcasted_iota(jnp.int32, (4 * per, gr), 0) % per
    r_col = lax.broadcasted_iota(jnp.int32, (4 * per, gr), 1)
    want = jnp.where(
        r_row < rows,
        r_row // AR + i * band_r,
        jnp.where(
            r_row == rows, i * band_r - 1, jnp.where(r_row == rows + 1, (i + 1) * band_r, -1)
        ),
    )
    r_sel = jnp.where(want == r_col, 1.0, 0.0)
    c_row = lax.broadcasted_iota(jnp.int32, (gr, nrad * cdev), 0)
    c_col = lax.broadcasted_iota(jnp.int32, (gr, nrad * cdev), 1)
    c_sel = jnp.where((c_col // cdev) * band_r + c_col % band_r == c_row, 1.0, 0.0)
    m_out = lax.broadcasted_iota(jnp.int32, (4 * per, nrad * cdev), 0) // per
    m_in = (lax.broadcasted_iota(jnp.int32, (4 * per, nrad * cdev), 1) % cdev) // band_r
    built = jnp.zeros((4 * per, nrad * cdev), jnp.float32)
    for h in range(2):
        for p in range(2):
            part = jnp.dot(
                jnp.dot(
                    r_sel, radial_ref[p, h], precision=HIGHEST, preferred_element_type=jnp.float32
                ),
                c_sel,
                precision=HIGHEST,
                preferred_element_type=jnp.float32,
            )
            if p == 0:
                built = jnp.where((m_out == m_in) & (m_out % 2 == h), part, built)
            else:
                built = jnp.where((m_out == h) & (m_in == 2 + h), -part, built)
                built = jnp.where((m_out == 2 + h) & (m_in == h), part, built)
    radmat[...] = built

    def mix_and_send(k):
        total = one_s[k]
        for d in range(1, nax):
            gather_one(k, d).wait_recv()
        for d in range(1, nax):
            total = total + one_r[k, lax.rem(j + d, nax)]
        outs = []
        for h in range(2):
            prod = lax.dot_general(
                total,
                axmat[h],
                (((1,), (1,)), ((), ())),
                precision=HIGHEST,
                preferred_element_type=jnp.float32,
            )
            a = prod[:, 0:lanes]
            b = prod[:, lanes : 2 * lanes]
            e = prod[:, 2 * lanes : 3 * lanes]
            f = pltpu.roll(e, half, 1)
            swap_b = pltpu.roll(b, rows // 2, 0)
            swap_f = pltpu.roll(f, rows // 2, 0)
            low = row < rows // 2
            outs.append(
                (jnp.where(low, a - swap_b, a + swap_b), jnp.where(low, e - swap_f, e + swap_f))
            )
        odd = (row // band_r) % 2 == 1
        two_r[k, i, :, 0:lanes] = jnp.where(odd, outs[1][0], outs[0][0])
        two_r[k, i, :, lanes : 2 * lanes] = jnp.where(odd, outs[1][1], outs[0][1])
        for d in range(1, nrad):
            gather_two(k, d).start()

    def finish_coarse(k):
        for d in range(1, nrad):
            gather_two(k, d).wait_recv()
        return jnp.dot(
            radmat[...],
            two_r[k].reshape(nrad * cdev, 2 * lanes),
            precision=HIGHEST,
            preferred_element_type=jnp.float32,
        )

    mix_and_send(0)
    on_faces(lambda d: stiff_copy(d ^ 1).wait_recv())

    mass = [mass_ref[0], mass_ref[1]]

    odd_lane = lane % 2 == 1

    def around(value, up, dn, beside, t):
        edge = pltpu.roll(beside, lanes - 1 - 2 * lax.rem(t, cap), 1)
        return (
            jnp.where(row == 0, up, pltpu.roll(value, 1, 0)),
            jnp.where(row == rows - 1, dn, pltpu.roll(value, rows - 1, 0)),
            pltpu.roll(jnp.where(lane == lanes - 1, edge, value), 1, 1),
            pltpu.roll(jnp.where(lane == 0, edge, value), lanes - 1, 1),
        )

    def put_rows(k, t, y):
        for c in range(4):
            row_s[k, 0, c, pl.ds(t, 1), :] = y[c][0:1]
            row_s[k, 1, c, pl.ds(t, 1), :] = y[c][rows - 1 : rows]

    def smooth(t, rr, ri, h):
        d_re, d_im, scale = dr[h, t], di[t], sc[h, t]
        return (d_re * rr + d_im * ri) * scale, (d_re * ri - d_im * rr) * scale

    for n in range(scol_s.shape[0]):
        col_m[0, n] = jnp.where(odd_lane, scol_r[1, n], scol_r[0, n])

    def setup_step(t, packs, beside):
        value = stiff[t + 1]
        up, dn, lo, hi = around(
            value,
            srow_r[0, pl.ds(t, 1), :],
            srow_r[1, pl.ds(t, 1), :],
            beside,
            t,
        )
        c_up, c_dn = 0.5 * (value + up), 0.5 * (value + dn)
        c_lo, c_hi = 0.5 * (value + lo), 0.5 * (value + hi)
        c_be, c_ah = 0.5 * (value + stiff[t]), 0.5 * (value + stiff[t + 2])
        wr_up[t] = c_up
        wr_dn[t] = c_dn
        wa_lo[t] = c_lo
        wa_hi[t] = c_hi
        wt[t] = c_be
        wt[t + 1] = c_ah
        total = c_dn + c_up + c_hi + c_lo + c_ah + c_be
        density = lookup(ids_ref[t], dens_ref)
        d_im = LOSS_FACTOR * total
        di[t] = d_im
        y = [None] * 4
        for h in range(2):
            d_re = total - mass[h] * density
            scale = RELAXATION / (d_re * d_re + d_im * d_im)
            dr[h, t] = d_re
            sc[h, t] = scale
            rr, ri = rhs_ref[0, h, t], rhs_ref[1, h, t]
            y[h] = (d_re * rr + d_im * ri) * scale
            y[2 + h] = (d_re * ri - d_im * rr) * scale
            sol_ref[0, h, t] = y[h]
            sol_ref[1, h, t] = y[2 + h]
        put_rows(0, t, y)
        return [pack(y[c], t, packs[c]) for c in range(4)]

    def setup_chunk(chunk, nothing):
        begin = chunk * CHUNK
        tile = begin // cap
        beside = col_m[0, tile]
        packs = [col_s[0, c, tile] for c in range(4)]
        for u in range(CHUNK):
            packs = setup_step(begin + u, packs, beside)
        for c in range(4):
            col_s[0, c, tile] = packs[c]
        return nothing

    lax.fori_loop(0, middle, setup_chunk, 0)
    on_faces(lambda d: halo_copy(0, d, 0).start(), 2)
    lax.fori_loop(middle, ct // CHUNK, setup_chunk, 0)
    on_faces(lambda d: halo_copy(0, d).start())

    cosines, sines = [], []
    for h in range(2):
        angle = jnp.full((rows, lanes), harm_ref[h], jnp.int32).astype(jnp.float32) * (
            2.0 * jnp.pi / NSECT
        )
        cosines.append(jnp.cos(angle))
        sines.append(jnp.sin(angle))

    for k in range(ITERS):
        final = k == ITERS - 1
        coarse = finish_coarse(k)
        corr = [coarse[c * per : c * per + rows, 0:lanes] for c in range(4)]
        on_faces(lambda d: halo_copy(k, d ^ 1, 0).wait_recv(), 2)
        on_faces(lambda d: halo_copy(k, d ^ 1).wait_recv())
        for c in range(4):
            add = []
            for side in range(2):
                at = c * per + rows + side
                row_r[k, side, c] = row_r[k, side, c] + coarse[at : at + 1, 0:lanes]
                add.append(coarse[c * per : c * per + rows, lanes + side : lanes + side + 1])
            for n in range(col_m.shape[1]):
                col_m[c, n] = jnp.where(
                    odd_lane, col_r[k, 1, c, n] + add[1], col_r[k, 0, c, n] + add[0]
                )

        def load(t):
            return [sol_ref[c // 2, c % 2, t] + corr[c] for c in range(4)]

        def turn(x, sign):
            return [cosines[h] * x[h] - sign * sines[h] * x[2 + h] for h in range(2)] + [
                sign * sines[h] * x[h] + cosines[h] * x[2 + h] for h in range(2)
            ]

        start = load(0)
        beyond = turn(start, 1.0)
        before = turn(load(ct - 1), -1.0)

        def stencil(t, xm, x, xp, beside):
            c_up, c_dn, c_lo, c_hi = wr_up[t], wr_dn[t], wa_lo[t], wa_hi[t]
            c_be, c_ah = wt[t], wt[t + 1]
            nb = []
            for c in range(4):
                up, dn, lo, hi = around(
                    x[c],
                    row_r[k, 0, c, pl.ds(t, 1), :],
                    row_r[k, 1, c, pl.ds(t, 1), :],
                    beside[c],
                    t,
                )
                nb.append(
                    (c_dn * dn + c_up * up)
                    + (c_hi * hi + c_lo * lo)
                    + (c_ah * xp[c] + c_be * xm[c])
                )
            d_im = di[t]
            res = [None] * 4
            for h in range(2):
                d_re = dr[h, t]
                re, im = h, 2 + h
                res[re] = rhs_ref[0, h, t] - (
                    d_re * x[re] - d_im * x[im] - (nb[re] - LOSS_FACTOR * nb[im])
                )
                res[im] = rhs_ref[1, h, t] - (
                    d_re * x[im] + d_im * x[re] - (nb[im] + LOSS_FACTOR * nb[re])
                )
            return res

        def chunk_pass(chunk, carry):
            xm, x, sums = list(carry[0:4]), list(carry[4:8]), list(carry[8:])
            begin = chunk * CHUNK
            tile = begin // cap
            beside = [col_m[c, tile] for c in range(4)]
            if not final:
                packs = [col_s[k + 1, c, tile] for c in range(4)]
            for u in range(CHUNK):
                t = begin + u
                if u < CHUNK - 1:
                    xp = load(t + 1)
                else:
                    ended = t == ct - 1
                    xp = load(jnp.minimum(t + 1, ct - 1))
                    xp = [jnp.where(ended, beyond[c], xp[c]) for c in range(4)]
                res = stencil(t, xm, x, xp, beside)
                if final:
                    for c in range(4):
                        sol_ref[c // 2, c % 2, t] = x[c]
                        res_ref[c // 2, c % 2, t] = res[c]
                else:
                    y = [None] * 4
                    for h in range(2):
                        a, b = smooth(t, res[h], res[2 + h], h)
                        y[h], y[2 + h] = x[h] + a, x[2 + h] + b
                    for c in range(4):
                        sol_ref[c // 2, c % 2, t] = y[c]
                        sums[c] = sums[c] + res[c]
                        packs[c] = pack(y[c], t, packs[c])
                    put_rows(k + 1, t, y)
                xm, x = x, xp
            if not final:
                for c in range(4):
                    col_s[k + 1, c, tile] = packs[c]
            return tuple(xm) + tuple(x) + tuple(sums)

        state = () if final else (zero,) * 4
        carry = tuple(before) + tuple(start) + state
        if final:
            lax.fori_loop(0, ct // CHUNK, chunk_pass, carry)
        else:
            carry = lax.fori_loop(0, middle, chunk_pass, carry)
            on_faces(lambda d: halo_copy(k + 1, d, 0).start(), 2)
            carry = lax.fori_loop(middle, ct // CHUNK, chunk_pass, carry)
        if not final:
            restrict_and_send(k + 1, carry[8:])
            on_faces(lambda d: halo_copy(k + 1, d).start())
            mix_and_send(k + 1)

    on_faces(lambda d: stiff_copy(d).wait_send())
    for k in range(ITERS):
        on_faces(lambda d: halo_copy(k, d, 0).wait_send(), 2)
        on_faces(lambda d: halo_copy(k, d).wait_send())
        for d in range(1, nax):
            gather_one(k, d).wait_send()
        for d in range(1, nrad):
            gather_two(k, d).wait_send()


def local(rhs, mat_ids, stiff_table, dens_table, mass_shift, harmonic, radial_factor, axial_factor):
    nrad = lax.axis_size("radial")
    nax = lax.axis_size("axial")
    ct, rows, lanes = mat_ids.shape
    vmem = pl.BlockSpec(memory_space=pltpu.VMEM)
    hbm = pl.BlockSpec(memory_space=pltpu.HBM)
    tiles = -(-2 * ct // lanes)
    f32 = jnp.float32
    field = (ct, rows, lanes)
    cdev = 4 * (rows // AR)
    dma = pltpu.SemaphoreType.DMA
    return pl.pallas_call(
        functools.partial(kernel, nrad, nax),
        out_shape=(jax.ShapeDtypeStruct(rhs.shape, f32), jax.ShapeDtypeStruct(rhs.shape, f32)),
        in_specs=[hbm] * 8,
        out_specs=(vmem, vmem),
        scratch_shapes=[
            pltpu.VMEM(rhs.shape, f32),
            pltpu.VMEM(field, jnp.int32),
            pltpu.SMEM(stiff_table.shape, f32),
            pltpu.SMEM(dens_table.shape, f32),
            pltpu.SMEM(mass_shift.shape, f32),
            pltpu.SMEM(harmonic.shape, jnp.int32),
            pltpu.VMEM(radial_factor.shape, f32),
            pltpu.VMEM(axial_factor.shape, f32),
            dma((8,)),
            pltpu.VMEM((ct + 2, rows, lanes), f32),
            pltpu.VMEM(field, f32),
            pltpu.VMEM(field, f32),
            pltpu.VMEM(field, f32),
            pltpu.VMEM(field, f32),
            pltpu.VMEM((ct + 1, rows, lanes), f32),
            pltpu.VMEM((2,) + field, f32),
            pltpu.VMEM(field, f32),
            pltpu.VMEM((2,) + field, f32),
            pltpu.VMEM((2, ct, lanes), f32),
            pltpu.VMEM((2, ct, lanes), f32),
            pltpu.VMEM((tiles, rows, lanes), f32),
            pltpu.VMEM((2, tiles, rows, lanes), f32),
            pltpu.VMEM((ITERS, 2, 4, ct, lanes), f32),
            pltpu.VMEM((ITERS, 2, 4, ct, lanes), f32),
            pltpu.VMEM((ITERS, 4, tiles, rows, lanes), f32),
            pltpu.VMEM((ITERS, 2, 4, tiles, rows, lanes), f32),
            pltpu.VMEM((4, tiles, rows, lanes), f32),
            pltpu.VMEM((ITERS, rows, lanes), f32),
            pltpu.VMEM((ITERS, nax, rows, lanes), f32),
            pltpu.VMEM((ITERS, nrad, rows, 2 * lanes), f32),
            pltpu.VMEM((2, 3 * lanes, lanes), f32),
            pltpu.VMEM((8 * rows, nrad * cdev), f32),
            dma((4,)),
            dma((4,)),
            dma((ITERS, 2, 4)),
            dma((ITERS, 2, 4)),
            dma((ITERS, nax)),
            dma((ITERS, nax)),
            dma((ITERS, nrad)),
            dma((ITERS, nrad)),
        ],
        compiler_params=pltpu.CompilerParams(
            collective_id=0, has_side_effects=True, vmem_limit_bytes=58 * 1024 * 1024
        ),
    )(rhs, mat_ids, stiff_table, dens_table, mass_shift, harmonic, radial_factor, axial_factor)


def solution(mesh):
    return jax.shard_map(
        local,
        mesh=mesh,
        in_specs=(
            P(None, None, None, "radial", "axial"),
            P(None, "radial", "axial"),
            P(),
            P(),
            P(),
            P(),
            P(),
            P(),
        ),
        out_specs=(P(None, None, None, "radial", "axial"), P(None, None, None, "radial", "axial")),
        check_vma=False,
    )
```

```python
import functools

import jax
import jax.numpy as jnp
from jax import lax
from jax.experimental import pallas as pl
from jax.experimental.pallas import tpu as pltpu
from jax.sharding import PartitionSpec as P

ITERS = 3
NSECT = 24
AR = 4
AA = 8
LOSS_FACTOR = 0.2
RELAXATION = 0.6
MESH = pl.DeviceIdType.MESH
HIGHEST = lax.Precision.HIGHEST
CHUNK = 8


def kernel(
    nrad,
    nax,
    rhs_hbm,
    ids_hbm,
    stiff_hbm,
    dens_hbm,
    mass_hbm,
    harm_hbm,
    radial_hbm,
    axial_hbm,
    sol_ref,
    res_ref,
    rhs_ref,
    ids_ref,
    stiff_ref,
    dens_ref,
    mass_ref,
    harm_ref,
    radial_ref,
    axial_ref,
    in_sem,
    stiff,
    wr_up,
    wr_dn,
    wa_lo,
    wa_hi,
    wt,
    dr,
    di,
    sc,
    srow_s,
    srow_r,
    scol_s,
    scol_r,
    row_s,
    row_r,
    col_s,
    col_r,
    col_m,
    one_s,
    one_r,
    two_r,
    axmat,
    radmat,
    st_send,
    st_recv,
    ha_send,
    ha_recv,
    g1_send,
    g1_recv,
    g2_send,
    g2_recv,
):
    loads = [
        pltpu.make_async_copy(src, dst, in_sem.at[n])
        for n, (src, dst) in enumerate(
            (
                (stiff_hbm, stiff_ref),
                (ids_hbm, ids_ref),
                (rhs_hbm, rhs_ref),
                (dens_hbm, dens_ref),
                (mass_hbm, mass_ref),
                (harm_hbm, harm_ref),
                (radial_hbm, radial_ref),
                (axial_hbm, axial_ref),
            )
        )
    ]
    for load_in in loads:
        load_in.start()
    ct = rhs_ref.shape[2]
    rows, lanes = rhs_ref.shape[3:]
    gr = radial_ref.shape[2]
    ga = axial_ref.shape[2]
    band_r = rows // AR
    band_c = lanes // AA
    i = lax.axis_index("radial")
    j = lax.axis_index("axial")
    has_up, has_dn = i > 0, i < nrad - 1
    has_lo, has_hi = j > 0, j < nax - 1
    conds = (has_up, has_dn, has_lo, has_hi)
    targets = ({"radial": i - 1}, {"radial": i + 1}, {"axial": j - 1}, {"axial": j + 1})

    for d in range(4):

        @pl.when(jnp.logical_not(conds[d]))
        def _():
            if d < 2:
                srow_r[d] = jnp.zeros(srow_r.shape[1:], jnp.float32)
                for k in range(ITERS):
                    row_r[k, d] = jnp.zeros(row_r.shape[2:], jnp.float32)
            else:
                scol_r[d - 2] = jnp.zeros(scol_r.shape[1:], jnp.float32)
                for k in range(ITERS):
                    col_r[k, d - 2] = jnp.zeros(col_r.shape[2:], jnp.float32)

    barrier = pltpu.get_barrier_semaphore()
    for d in range(1, nax):
        pl.semaphore_signal(
            barrier, inc=1, device_id={"axial": lax.rem(j + d, nax)}, device_id_type=MESH
        )
    for d in range(1, nrad):
        pl.semaphore_signal(
            barrier, inc=1, device_id={"radial": lax.rem(i + d, nrad)}, device_id_type=MESH
        )

    row = lax.broadcasted_iota(jnp.int32, (rows, lanes), 0)
    lane = lax.broadcasted_iota(jnp.int32, (rows, lanes), 1)
    zero = jnp.zeros((rows, lanes), jnp.float32)

    def lookup(ids, table):
        value = jnp.full(ids.shape, table[0], jnp.float32)
        for entry in range(1, table.shape[0]):
            value = jnp.where(ids == entry, table[entry], value)
        return value

    cap = lanes // 2
    pair = lane // 2

    def pack(value, t, packed):
        at = lax.rem(t, cap)
        return jnp.where(pair == at, pltpu.roll(value, 2 * at + 1, 1), packed)

    def stiff_copy(d):
        if d < 2:
            src, dst = srow_s.at[d], srow_r.at[1 - d]
        else:
            src, dst = scol_s, scol_r.at[3 - d]
        return pltpu.make_async_remote_copy(
            src_ref=src,
            dst_ref=dst,
            send_sem=st_send.at[d],
            recv_sem=st_recv.at[d ^ 1],
            device_id=targets[d],
            device_id_type=MESH,
        )

    middle = 5 * (ct // CHUNK) // 6

    def halo_copy(k, d, late=1):
        if d < 2:
            part = pl.ds(middle * CHUNK, ct - middle * CHUNK) if late else pl.ds(0, middle * CHUNK)
            src, dst = row_s.at[k, d, :, part], row_r.at[k, 1 - d, :, part]
        else:
            src, dst = col_s.at[k], col_r.at[k, 3 - d]
        return pltpu.make_async_remote_copy(
            src_ref=src,
            dst_ref=dst,
            send_sem=ha_send.at[k, late, d],
            recv_sem=ha_recv.at[k, late, d ^ 1],
            device_id=targets[d],
            device_id_type=MESH,
        )

    def gather_one(k, d):
        return pltpu.make_async_remote_copy(
            src_ref=one_s.at[k],
            dst_ref=one_r.at[k, j],
            send_sem=g1_send.at[k, d],
            recv_sem=g1_recv.at[k, d],
            device_id={"axial": lax.rem(j + d, nax)},
            device_id_type=MESH,
        )

    def gather_two(k, d):
        return pltpu.make_async_remote_copy(
            src_ref=two_r.at[k, i],
            dst_ref=two_r.at[k, i],
            send_sem=g2_send.at[k, d],
            recv_sem=g2_recv.at[k, d],
            device_id={"radial": lax.rem(i + d, nrad)},
            device_id_type=MESH,
        )

    def on_faces(act, faces=4):
        for d in range(faces):

            @pl.when(conds[d])
            def _():
                act(d)

    scol_s[...] = jnp.zeros(scol_s.shape, jnp.float32)
    col_s[...] = jnp.zeros(col_s.shape, jnp.float32)
    loads[0].wait()
    loads[1].wait()

    @pl.loop(0, ct // CHUNK)
    def _(chunk):
        begin = chunk * CHUNK
        tile = begin // cap
        packed = scol_s[tile]
        for u in range(CHUNK):
            t = begin + u
            value = lookup(ids_ref[t], stiff_ref)
            stiff[t + 1] = value
            srow_s[0, pl.ds(t, 1), :] = value[0:1]
            srow_s[1, pl.ds(t, 1), :] = value[rows - 1 : rows]
            packed = pack(value, t, packed)
        scol_s[tile] = packed

    stiff[0] = stiff[ct]
    stiff[ct + 1] = stiff[1]

    pl.semaphore_wait(barrier, nax + nrad - 2)
    on_faces(lambda d: stiff_copy(d).start())

    e_row = lax.broadcasted_iota(jnp.int32, (lanes, lanes), 0)
    e_col = lax.broadcasted_iota(jnp.int32, (lanes, lanes), 1)
    fold = jnp.where(e_row // AA + j * band_c == e_col, 1.0, 0.0)

    def restrict_and_send(k, sums):
        tile = zero
        for c in range(4):
            s = sums[c] + pltpu.roll(sums[c], rows - 1, 0)
            s = s + pltpu.roll(s, rows - 2, 0)
            for g in range(band_r):
                to = c * band_r + g
                moved = pltpu.roll(s, (to - g * AR) % rows, 0)
                tile = jnp.where(row == to, moved, tile)
        one_s[k] = jnp.dot(tile, fold, precision=HIGHEST, preferred_element_type=jnp.float32)
        for d in range(1, nax):
            gather_one(k, d).start()

    loads[2].wait()

    def sum_pass(chunk, sums):
        sums = list(sums)
        for u in range(2 * CHUNK):
            for c in range(4):
                sums[c] = sums[c] + rhs_ref[c // 2, c % 2, chunk * 2 * CHUNK + u]
        return tuple(sums)

    restrict_and_send(0, lax.fori_loop(0, ct // (2 * CHUNK), sum_pass, (zero,) * 4))
    for load_in in loads[3:]:
        load_in.wait()

    ax_row = lax.broadcasted_iota(jnp.int32, (lanes, ga), 0)
    ax_col = lax.broadcasted_iota(jnp.int32, (lanes, ga), 1)
    own = jnp.where(ax_row // AA + j * band_c == ax_col, 1.0, 0.0)
    edge_lo = j * band_c - 1
    edge_hi = (j + 1) * band_c
    half = lanes // 2
    edges = []
    for p in range(2):
        hit = ((ax_row == p * half) & (ax_col == edge_lo)) | (
            (ax_row == p * half + 1) & (ax_col == edge_hi)
        )
        edges.append(jnp.where(hit, 1.0, 0.0))
    for h in range(2):
        if ga < lanes:
            axmat[h] = jnp.zeros(axmat.shape[1:], jnp.float32)

        def spread(select, p):
            return jnp.dot(
                select, axial_ref[p, h], precision=HIGHEST, preferred_element_type=jnp.float32
            )

        axmat[h, 0:lanes, 0:ga] = spread(own, 0)
        axmat[h, lanes : 2 * lanes, 0:ga] = spread(own, 1)
        axmat[h, 2 * lanes : 3 * lanes, 0:ga] = spread(edges[0], 0) + spread(edges[1], 1)

    per = 2 * rows
    cdev = 4 * band_r
    r_row = lax.broadcasted_iota(jnp.int32, (4 * per, gr), 0) % per
    r_col = lax.broadcasted_iota(jnp.int32, (4 * per, gr), 1)
    want = jnp.where(
        r_row < rows,
        r_row // AR + i * band_r,
        jnp.where(
            r_row == rows, i * band_r - 1, jnp.where(r_row == rows + 1, (i + 1) * band_r, -1)
        ),
    )
    r_sel = jnp.where(want == r_col, 1.0, 0.0)
    c_row = lax.broadcasted_iota(jnp.int32, (gr, nrad * cdev), 0)
    c_col = lax.broadcasted_iota(jnp.int32, (gr, nrad * cdev), 1)
    c_sel = jnp.where((c_col // cdev) * band_r + c_col % band_r == c_row, 1.0, 0.0)
    m_out = lax.broadcasted_iota(jnp.int32, (4 * per, nrad * cdev), 0) // per
    m_in = (lax.broadcasted_iota(jnp.int32, (4 * per, nrad * cdev), 1) % cdev) // band_r
    built = jnp.zeros((4 * per, nrad * cdev), jnp.float32)
    for h in range(2):
        for p in range(2):
            part = jnp.dot(
                jnp.dot(
                    r_sel, radial_ref[p, h], precision=HIGHEST, preferred_element_type=jnp.float32
                ),
                c_sel,
                precision=HIGHEST,
                preferred_element_type=jnp.float32,
            )
            if p == 0:
                built = jnp.where((m_out == m_in) & (m_out % 2 == h), part, built)
            else:
                built = jnp.where((m_out == h) & (m_in == 2 + h), -part, built)
                built = jnp.where((m_out == 2 + h) & (m_in == h), part, built)
    radmat[...] = built

    def mix_and_send(k):
        total = one_s[k]
        for d in range(1, nax):
            gather_one(k, d).wait_recv()
        for d in range(1, nax):
            total = total + one_r[k, lax.rem(j + d, nax)]
        outs = []
        for h in range(2):
            prod = lax.dot_general(
                total,
                axmat[h],
                (((1,), (1,)), ((), ())),
                precision=HIGHEST,
                preferred_element_type=jnp.float32,
            )
            a = prod[:, 0:lanes]
            b = prod[:, lanes : 2 * lanes]
            e = prod[:, 2 * lanes : 3 * lanes]
            f = pltpu.roll(e, half, 1)
            swap_b = pltpu.roll(b, rows // 2, 0)
            swap_f = pltpu.roll(f, rows // 2, 0)
            low = row < rows // 2
            outs.append(
                (jnp.where(low, a - swap_b, a + swap_b), jnp.where(low, e - swap_f, e + swap_f))
            )
        odd = (row // band_r) % 2 == 1
        two_r[k, i, :, 0:lanes] = jnp.where(odd, outs[1][0], outs[0][0])
        two_r[k, i, :, lanes : 2 * lanes] = jnp.where(odd, outs[1][1], outs[0][1])
        for d in range(1, nrad):
            gather_two(k, d).start()

    def finish_coarse(k):
        for d in range(1, nrad):
            gather_two(k, d).wait_recv()
        return jnp.dot(
            radmat[...],
            two_r[k].reshape(nrad * cdev, 2 * lanes),
            precision=HIGHEST,
            preferred_element_type=jnp.float32,
        )

    mix_and_send(0)
    on_faces(lambda d: stiff_copy(d ^ 1).wait_recv())

    mass = [mass_ref[0], mass_ref[1]]

    odd_lane = lane % 2 == 1

    def around(value, up, dn, beside, t):
        edge = pltpu.roll(beside, lanes - 1 - 2 * lax.rem(t, cap), 1)
        return (
            jnp.where(row == 0, up, pltpu.roll(value, 1, 0)),
            jnp.where(row == rows - 1, dn, pltpu.roll(value, rows - 1, 0)),
            pltpu.roll(jnp.where(lane == lanes - 1, edge, value), 1, 1),
            pltpu.roll(jnp.where(lane == 0, edge, value), lanes - 1, 1),
        )

    def put_rows(k, t, y):
        for c in range(4):
            row_s[k, 0, c, pl.ds(t, 1), :] = y[c][0:1]
            row_s[k, 1, c, pl.ds(t, 1), :] = y[c][rows - 1 : rows]

    def smooth(t, rr, ri, h):
        d_re, d_im, scale = dr[h, t], di[t], sc[h, t]
        return (d_re * rr + d_im * ri) * scale, (d_re * ri - d_im * rr) * scale

    for n in range(scol_s.shape[0]):
        col_m[0, n] = jnp.where(odd_lane, scol_r[1, n], scol_r[0, n])

    def setup_step(t, packs, beside):
        value = stiff[t + 1]
        up, dn, lo, hi = around(
            value,
            srow_r[0, pl.ds(t, 1), :],
            srow_r[1, pl.ds(t, 1), :],
            beside,
            t,
        )
        c_up, c_dn = 0.5 * (value + up), 0.5 * (value + dn)
        c_lo, c_hi = 0.5 * (value + lo), 0.5 * (value + hi)
        c_be, c_ah = 0.5 * (value + stiff[t]), 0.5 * (value + stiff[t + 2])
        wr_up[t] = c_up
        wr_dn[t] = c_dn
        wa_lo[t] = c_lo
        wa_hi[t] = c_hi
        wt[t] = c_be
        wt[t + 1] = c_ah
        total = c_dn + c_up + c_hi + c_lo + c_ah + c_be
        density = lookup(ids_ref[t], dens_ref)
        d_im = LOSS_FACTOR * total
        di[t] = d_im
        y = [None] * 4
        for h in range(2):
            d_re = total - mass[h] * density
            scale = RELAXATION / (d_re * d_re + d_im * d_im)
            dr[h, t] = d_re
            sc[h, t] = scale
            rr, ri = rhs_ref[0, h, t], rhs_ref[1, h, t]
            y[h] = (d_re * rr + d_im * ri) * scale
            y[2 + h] = (d_re * ri - d_im * rr) * scale
            sol_ref[0, h, t] = y[h]
            sol_ref[1, h, t] = y[2 + h]
        put_rows(0, t, y)
        return [pack(y[c], t, packs[c]) for c in range(4)]

    def setup_chunk(chunk, nothing):
        begin = chunk * CHUNK
        tile = begin // cap
        beside = col_m[0, tile]
        packs = [col_s[0, c, tile] for c in range(4)]
        for u in range(CHUNK):
            packs = setup_step(begin + u, packs, beside)
        for c in range(4):
            col_s[0, c, tile] = packs[c]
        return nothing

    lax.fori_loop(0, middle, setup_chunk, 0)
    on_faces(lambda d: halo_copy(0, d, 0).start(), 2)
    lax.fori_loop(middle, ct // CHUNK, setup_chunk, 0)
    on_faces(lambda d: halo_copy(0, d).start())

    cosines, sines = [], []
    for h in range(2):
        angle = jnp.full((rows, lanes), harm_ref[h], jnp.int32).astype(jnp.float32) * (
            2.0 * jnp.pi / NSECT
        )
        cosines.append(jnp.cos(angle))
        sines.append(jnp.sin(angle))

    for k in range(ITERS):
        final = k == ITERS - 1
        coarse = finish_coarse(k)
        corr = [coarse[c * per : c * per + rows, 0:lanes] for c in range(4)]
        on_faces(lambda d: halo_copy(k, d ^ 1, 0).wait_recv(), 2)
        on_faces(lambda d: halo_copy(k, d ^ 1).wait_recv())
        for c in range(4):
            add = []
            for side in range(2):
                at = c * per + rows + side
                row_r[k, side, c] = row_r[k, side, c] + coarse[at : at + 1, 0:lanes]
                add.append(coarse[c * per : c * per + rows, lanes + side : lanes + side + 1])
            for n in range(col_m.shape[1]):
                col_m[c, n] = jnp.where(
                    odd_lane, col_r[k, 1, c, n] + add[1], col_r[k, 0, c, n] + add[0]
                )

        def load(t):
            return [sol_ref[c // 2, c % 2, t] + corr[c] for c in range(4)]

        def turn(x, sign):
            return [cosines[h] * x[h] - sign * sines[h] * x[2 + h] for h in range(2)] + [
                sign * sines[h] * x[h] + cosines[h] * x[2 + h] for h in range(2)
            ]

        start = load(0)
        beyond = turn(start, 1.0)
        before = turn(load(ct - 1), -1.0)

        def stencil(t, xm, x, xp, beside):
            c_up, c_dn, c_lo, c_hi = wr_up[t], wr_dn[t], wa_lo[t], wa_hi[t]
            c_be, c_ah = wt[t], wt[t + 1]
            nb = []
            for c in range(4):
                up, dn, lo, hi = around(
                    x[c],
                    row_r[k, 0, c, pl.ds(t, 1), :],
                    row_r[k, 1, c, pl.ds(t, 1), :],
                    beside[c],
                    t,
                )
                nb.append(
                    (c_dn * dn + c_up * up)
                    + (c_hi * hi + c_lo * lo)
                    + (c_ah * xp[c] + c_be * xm[c])
                )
            d_im = di[t]
            res = [None] * 4
            for h in range(2):
                d_re = dr[h, t]
                re, im = h, 2 + h
                res[re] = rhs_ref[0, h, t] - (
                    d_re * x[re] - d_im * x[im] - (nb[re] - LOSS_FACTOR * nb[im])
                )
                res[im] = rhs_ref[1, h, t] - (
                    d_re * x[im] + d_im * x[re] - (nb[im] + LOSS_FACTOR * nb[re])
                )
            return res

        def chunk_pass(chunk, carry):
            xm, x, sums = list(carry[0:4]), list(carry[4:8]), list(carry[8:])
            begin = chunk * CHUNK
            tile = begin // cap
            beside = [col_m[c, tile] for c in range(4)]
            if not final:
                packs = [col_s[k + 1, c, tile] for c in range(4)]
            for u in range(CHUNK):
                t = begin + u
                if u < CHUNK - 1:
                    xp = load(t + 1)
                else:
                    ended = t == ct - 1
                    xp = load(jnp.minimum(t + 1, ct - 1))
                    xp = [jnp.where(ended, beyond[c], xp[c]) for c in range(4)]
                res = stencil(t, xm, x, xp, beside)
                if final:
                    for c in range(4):
                        sol_ref[c // 2, c % 2, t] = x[c]
                        res_ref[c // 2, c % 2, t] = res[c]
                else:
                    y = [None] * 4
                    for h in range(2):
                        a, b = smooth(t, res[h], res[2 + h], h)
                        y[h], y[2 + h] = x[h] + a, x[2 + h] + b
                    for c in range(4):
                        sol_ref[c // 2, c % 2, t] = y[c]
                        sums[c] = sums[c] + res[c]
                        packs[c] = pack(y[c], t, packs[c])
                    put_rows(k + 1, t, y)
                xm, x = x, xp
            if not final:
                for c in range(4):
                    col_s[k + 1, c, tile] = packs[c]
            return tuple(xm) + tuple(x) + tuple(sums)

        state = () if final else (zero,) * 4
        carry = tuple(before) + tuple(start) + state
        if final:
            lax.fori_loop(0, ct // CHUNK, chunk_pass, carry)
        else:
            carry = lax.fori_loop(0, middle, chunk_pass, carry)
            on_faces(lambda d: halo_copy(k + 1, d, 0).start(), 2)
            carry = lax.fori_loop(middle, ct // CHUNK, chunk_pass, carry)
        if not final:
            restrict_and_send(k + 1, carry[8:])
            on_faces(lambda d: halo_copy(k + 1, d).start())
            mix_and_send(k + 1)

    on_faces(lambda d: stiff_copy(d).wait_send())
    for k in range(ITERS):
        on_faces(lambda d: halo_copy(k, d, 0).wait_send(), 2)
        on_faces(lambda d: halo_copy(k, d).wait_send())
        for d in range(1, nax):
            gather_one(k, d).wait_send()
        for d in range(1, nrad):
            gather_two(k, d).wait_send()


def local(rhs, mat_ids, stiff_table, dens_table, mass_shift, harmonic, radial_factor, axial_factor):
    nrad = lax.axis_size("radial")
    nax = lax.axis_size("axial")
    ct, rows, lanes = mat_ids.shape
    vmem = pl.BlockSpec(memory_space=pltpu.VMEM)
    hbm = pl.BlockSpec(memory_space=pltpu.HBM)
    tiles = -(-2 * ct // lanes)
    f32 = jnp.float32
    field = (ct, rows, lanes)
    cdev = 4 * (rows // AR)
    dma = pltpu.SemaphoreType.DMA
    return pl.pallas_call(
        functools.partial(kernel, nrad, nax),
        out_shape=(jax.ShapeDtypeStruct(rhs.shape, f32), jax.ShapeDtypeStruct(rhs.shape, f32)),
        in_specs=[hbm] * 8,
        out_specs=(vmem, vmem),
        scratch_shapes=[
            pltpu.VMEM(rhs.shape, f32),
            pltpu.VMEM(field, jnp.int32),
            pltpu.SMEM(stiff_table.shape, f32),
            pltpu.SMEM(dens_table.shape, f32),
            pltpu.SMEM(mass_shift.shape, f32),
            pltpu.SMEM(harmonic.shape, jnp.int32),
            pltpu.VMEM(radial_factor.shape, f32),
            pltpu.VMEM(axial_factor.shape, f32),
            dma((8,)),
            pltpu.VMEM((ct + 2, rows, lanes), f32),
            pltpu.VMEM(field, f32),
            pltpu.VMEM(field, f32),
            pltpu.VMEM(field, f32),
            pltpu.VMEM(field, f32),
            pltpu.VMEM((ct + 1, rows, lanes), f32),
            pltpu.VMEM((2,) + field, f32),
            pltpu.VMEM(field, f32),
            pltpu.VMEM((2,) + field, f32),
            pltpu.VMEM((2, ct, lanes), f32),
            pltpu.VMEM((2, ct, lanes), f32),
            pltpu.VMEM((tiles, rows, lanes), f32),
            pltpu.VMEM((2, tiles, rows, lanes), f32),
            pltpu.VMEM((ITERS, 2, 4, ct, lanes), f32),
            pltpu.VMEM((ITERS, 2, 4, ct, lanes), f32),
            pltpu.VMEM((ITERS, 4, tiles, rows, lanes), f32),
            pltpu.VMEM((ITERS, 2, 4, tiles, rows, lanes), f32),
            pltpu.VMEM((4, tiles, rows, lanes), f32),
            pltpu.VMEM((ITERS, rows, lanes), f32),
            pltpu.VMEM((ITERS, nax, rows, lanes), f32),
            pltpu.VMEM((ITERS, nrad, rows, 2 * lanes), f32),
            pltpu.VMEM((2, 3 * lanes, lanes), f32),
            pltpu.VMEM((8 * rows, nrad * cdev), f32),
            dma((4,)),
            dma((4,)),
            dma((ITERS, 2, 4)),
            dma((ITERS, 2, 4)),
            dma((ITERS, nax)),
            dma((ITERS, nax)),
            dma((ITERS, nrad)),
            dma((ITERS, nrad)),
        ],
        compiler_params=pltpu.CompilerParams(
            collective_id=0, has_side_effects=True, vmem_limit_bytes=58 * 1024 * 1024
        ),
    )(rhs, mat_ids, stiff_table, dens_table, mass_shift, harmonic, radial_factor, axial_factor)


def solution(mesh):
    return jax.shard_map(
        local,
        mesh=mesh,
        in_specs=(
            P(None, None, None, "radial", "axial"),
            P(None, "radial", "axial"),
            P(),
            P(),
            P(),
            P(),
            P(),
            P(),
        ),
        out_specs=(P(None, None, None, "radial", "axial"), P(None, None, None, "radial", "axial")),
        check_vma=False,
    )
```
